256 devices in a mesh: chol: 16 (over x_lo, y, core), orb: 16 (over x_hi, z).
Axes of the slice: x: 4 (x_hi: 2, x_lo: 2; x = x_hi * 2 + x_lo), y: 4, z: 8, core: 2. Of those that a mesh axis runs over, the one named last changes fastest.
Arguments:
- phi_walkers: bfloat16 [16, 200, 1024], P('chol', None, 'orb'), may hold values from -6 to 6
- theta_half: bfloat16 [16, 200, 1024], P(None, None, 'orb'), may hold values from -0.5 to 0.5
- chol_vectors: bfloat16 [1024, 1024, 1024], P('chol', 'orb'), may hold values from -0.0034179688 to 0.0034179688
- chol_rotated: bfloat16 [1024, 200, 1024], P('chol', None, 'orb'), may hold values from -0.4375 to 0.4375
- hcore_rotated: bfloat16 [200, 1024], P(None, 'orb'), may hold values from -0.5 to 0.5
- aux_fields: float32 [16, 1024], P(None, 'chol'), may hold values from -6 to 6
Outputs:
- walkers_out: bfloat16 [16, 200, 1024], P('chol', None, 'orb')
- energy: float32 [16], replicated
The draws below stay inside these ranges and needn't reach their ends.
All inputs are finite; a program needn't handle non-finite values.
Results may differ from the reference program's by a relative error of at most 0.013.
Values may be sent and summed in bfloat16 or wider, within the bound.
A program may use at most 128 MiB of HBM per device.

```python
import jax
import jax.numpy as jnp
from jax import lax

NORB = 1024
NELEC = 200
CHOL_DEV = 64
ORDER = 4
NCHOL = 1024
WALKERS = 16


def block_scale(rng, dims, split, least, largest):
    loudness, own = 1.0, jax.random.fold_in(rng, 6)
    for dim, parts in split:
        draws = jnp.exp(jax.random.uniform(jax.random.fold_in(own, dim), (parts,), jnp.float32, least / len(split), largest / len(split)))
        loudness = loudness * jnp.repeat(draws, dims[dim] // parts).reshape([-1 if axis == dim else 1 for axis in range(len(dims))])
    return loudness


def normal_values(stream_key, shape, deviation, reach, pieces=(), held_as=jnp.bfloat16):
    result = jax.random.normal(stream_key, shape, jnp.float32) * deviation
    if len(pieces) > 0:
        result = block_scale(stream_key, shape, pieces, -0.22, 0.18) * result
    return jnp.clip(result, min=-reach, max=reach).astype(held_as)


def setup_inputs(seed: int = 0) -> dict:
    key_of = jax.random.split(jax.random.key(seed), 7)
    phi_walkers = normal_values(key_of[0], (WALKERS, NELEC, NORB), 1.0, 6.0, ((0, 16), (2, 16)))
    theta_half = normal_values(key_of[1], (WALKERS, NELEC, NORB), 0.0625, 0.5, ((2, 16),))
    chol_vectors = normal_values(key_of[2], (NCHOL, NORB, NORB), (25 * NORB * NCHOL // 8) ** -0.5, 0.0034179688, ((0, 16), (1, 16)))
    chol_rotated = normal_values(key_of[3], (NCHOL, NELEC, NORB), NELEC ** -0.5, 0.4375, ((0, 16), (2, 16)))
    hcore_rotated = normal_values(key_of[4], (NELEC, NORB), 0.07, 0.5, ((1, 16),))
    aux_fields = normal_values(key_of[5], (WALKERS, NCHOL), 1.0, 6.0, ((1, 16),), jnp.float32)
    return dict(phi_walkers=phi_walkers, theta_half=theta_half, chol_vectors=chol_vectors, chol_rotated=chol_rotated, hcore_rotated=hcore_rotated, aux_fields=aux_fields)


def reference(phi_walkers, theta_half, chol_vectors, chol_rotated, hcore_rotated, aux_fields):
    walkers_all = theta_half.shape[0]
    flat_theta = theta_half.reshape(walkers_all, -1)
    force_bias = jnp.dot(flat_theta, chol_rotated.reshape(NCHOL, -1).T, preferred_element_type=jnp.float32)
    one_body = jnp.dot(flat_theta, hcore_rotated.reshape(-1), preferred_element_type=jnp.float32)
    shifted = (aux_fields - force_bias).astype(jnp.bfloat16)
    operator = jnp.dot(shifted, chol_vectors.reshape(NCHOL, -1), preferred_element_type=jnp.float32)
    operator = operator.astype(jnp.bfloat16).reshape(walkers_all, NORB, NORB)
    operator_wide = operator.astype(jnp.float32)
    current = phi_walkers
    accumulated = phi_walkers.astype(jnp.float32)
    for degree in range(1, ORDER + 1):
        product = jnp.einsum('weq,wpq->wep', current.astype(jnp.float32), operator_wide)
        current = (product / degree).astype(jnp.bfloat16)
        accumulated = accumulated + current.astype(jnp.float32)
    walkers_out = accumulated.astype(jnp.bfloat16)
    theta_wide = theta_half.astype(jnp.float32)
    blocks = chol_rotated.reshape(NCHOL // CHOL_DEV, CHOL_DEV, NELEC, NORB)

    def block_pairs(vector_block):
        pair_matrix = jnp.einsum('aen,wfn->awef', vector_block.astype(jnp.float32), theta_wide)
        return jnp.einsum('awef,awfe->w', pair_matrix, pair_matrix)

    pairs_sum = jnp.sum(lax.map(block_pairs, blocks), axis=0)
    coulomb = jnp.sum(force_bias * force_bias, axis=1)
    energy = one_body + (0.5 / NCHOL) * (coulomb - pairs_sum)
    return walkers_out, energy
```

```python
import jax
import jax.numpy as jnp
from jax import lax
from jax.experimental import pallas as pl
from jax.experimental.pallas import tpu as pltpu
from jax.sharding import PartitionSpec as P

ORDER = 4
MESH = pl.DeviceIdType.MESH
F32 = jnp.float32
BF16 = jnp.bfloat16
VECTORS = 1024
TILE = 16


def iota(shape, dim):
    return lax.broadcasted_iota(jnp.int32, shape, dim)


def kernel(phi, th, cv, cr, hc, aux, wout, en,
           crv, cvv, thv, tbuf, abuf, a_t, fbx, smat, opart, osib, osum, opl, obuf, ored,
           pbuf, term, acc, res, land, x_buf, ebuf, e2buf,
           s_loc, s_t1, r_t1, s_tx, r_tx, s_ty, r_ty, s_tf, r_tf, s_phi, r_phi,
           s_a, r_a, s_as, r_as, s_fb, r_fb, s_os, r_os, s_op, r_op, s_od, r_od,
           s_w, r_w, s_e1, r_e1, s_e2, r_e2):
    c = lax.axis_index("chol")
    o = lax.axis_index("orb")
    core = lax.rem(c, 2)
    xl = c // 8
    y = lax.rem(c // 2, 4)
    j = c // 2
    sib = (2 * j + 1 - core, o)
    yp = lax.rem(y + 1, 4)
    ym = lax.rem(y + 3, 4)
    y2 = lax.rem(y + 2, 4)

    def plane(jj):
        return (2 * jj + core, o)

    xpart = plane((1 - xl) * 4 + y)
    dest = core * 8 + lax.rem(2 * y + xl + 4 * core, 8)

    def rcopy(src, dst, ss, rs, dev):
        return pltpu.make_async_remote_copy(
            src_ref=src, dst_ref=dst, send_sem=ss, recv_sem=rs, device_id=dev, device_id_type=MESH)

    def orb_peer(i):
        return lax.rem(o + i, 16)

    def plane_peer(i):
        return lax.rem(j + i, 8)

    cp_cr = pltpu.make_async_copy(cr, crv, s_loc.at[0])
    cp_cr.start()
    cp_th = pltpu.make_async_copy(th, thv, s_loc.at[1])
    cp_th.start()
    cp_cv = pltpu.make_async_copy(cv, cvv, s_loc.at[2])
    cp_cv.start()

    bar = pltpu.get_barrier_semaphore()

    def sig_orb(i, _):
        pl.semaphore_signal(bar, inc=1, device_id=(c, orb_peer(i)), device_id_type=MESH)
        return 0

    def sig_chol(i, _):
        pl.semaphore_signal(bar, inc=1, device_id=(lax.rem(c + i, 16), o), device_id_type=MESH)
        return 0

    lax.fori_loop(1, 16, sig_orb, 0)
    lax.fori_loop(1, 16, sig_chol, 0)
    pl.semaphore_wait(bar, 30)

    cp_own_t = pltpu.make_async_copy(th.at[c], tbuf.at[j, o], s_loc.at[3])
    cp_own_t.start()

    def t1(i):
        return rcopy(th.at[c], tbuf.at[j, o], s_t1.at[i], r_t1.at[o], (c, orb_peer(i)))

    def t1_start(i, _):
        t1(i).start()
        return 0

    lax.fori_loop(1, 16, t1_start, 0)

    cp_phi = rcopy(phi, pbuf.at[o], s_phi, r_phi.at[o], (c, dest))
    cp_phi_own = pltpu.make_async_copy(phi, pbuf.at[o], s_loc.at[4])

    @pl.when(o != dest)
    def _():
        cp_phi.start()

    @pl.when(o == dest)
    def _():
        cp_phi_own.start()

    def a2a(i):
        p = orb_peer(i)
        return rcopy(cr.at[pl.ds(4 * p, 4)], abuf.at[core, o], s_a.at[i], r_a.at[o], (c, p))

    def a2a_start(i, _):
        a2a(i).start()
        return 0

    cp_own_a = pltpu.make_async_copy(cr.at[pl.ds(4 * o, 4)], abuf.at[core, o], s_loc.at[5])
    cp_own_a.start()

    cp_th.wait()
    cp_cr.wait()
    mask = (iota((64, 256), 0) == lax.rem(iota((64, 256), 1), 64)).astype(F32)

    def split_dot(z, ind):
        hi = z.astype(BF16)
        lo = (z - hi.astype(F32)).astype(BF16)
        return (jnp.dot(hi, ind, preferred_element_type=F32)
                + jnp.dot(lo, ind, preferred_element_type=F32))

    def fb_step(i, tot):
        rhs = crv[pl.ds(4 * i, 4)].reshape(256, 200)
        z = lax.dot_general(thv[...].reshape(1024, 200), rhs, (((1,), (1,)), ((), ())),
                            preferred_element_type=F32)
        z = jnp.sum(z.reshape(16, 64, 256) * mask[None], axis=1)
        ind = (iota((256, 128), 1) == 4 * i + iota((256, 128), 0) // 64).astype(BF16)
        return tot + split_dot(z, ind)

    fb_part = lax.fori_loop(0, 16, fb_step, jnp.zeros((16, 128), F32))
    z1 = lax.dot_general(thv[...].reshape(1024, 200), hc[...], (((1,), (1,)), ((), ())),
                         preferred_element_type=F32)
    z1 = jnp.sum(z1.reshape(16, 64, 64) * mask[None, :, :64], axis=1)
    one_part = jnp.sum(z1, axis=1, keepdims=True)
    fbx[o] = fb_part + jnp.where(iota((16, 128), 1) == 64, one_part, 0.0)

    def fb_copy(i):
        return rcopy(fbx.at[o], fbx.at[o], s_fb.at[i], r_fb.at[o], (c, orb_peer(i)))

    def fb_start(i, _):
        fb_copy(i).start()
        return 0

    lax.fori_loop(1, 16, fb_start, 0)
    lax.fori_loop(1, 16, a2a_start, 0)

    def fb_wait(i, _):
        p = orb_peer(i)
        rcopy(fbx.at[p], fbx.at[p], s_fb.at[i], r_fb.at[p], (c, p)).wait_recv()
        return 0

    lax.fori_loop(1, 16, fb_wait, 0)
    fb_all = jnp.sum(fbx[...], axis=0)
    shifted = (aux[...] - fb_all[:, :64]).astype(BF16)

    row = iota((256, 16), 0)
    ew = (iota((256, 16), 1) == 2 * lax.rem(row // TILE, 8) + row // 128).astype(BF16)
    ea = (iota((64, 1024), 0) == iota((64, 1024), 1) // TILE).astype(BF16)
    spread = jnp.dot(jnp.dot(ew, shifted, preferred_element_type=F32).astype(BF16), ea,
                     preferred_element_type=F32)
    diag = lax.rem(iota((256, 1024), 0), TILE) == lax.rem(iota((256, 1024), 1), TILE)
    smat[...] = jnp.where(diag, spread, 0.0).astype(BF16)
    cp_cv.wait()

    def os_copy(t):
        return rcopy(opart.at[t, 1 - core], osib.at[t], s_os.at[t], r_os.at[t], sib)

    def op_step(t, _):
        def op_half(h, _):
            cols = pl.ds(pl.multiple_of(h * 256, 256), 256)
            rt = cvv[:, pl.ds(pl.multiple_of(TILE * t, TILE), TILE), cols].reshape(1024, 256)
            opart[t, :, :, :, cols] = jnp.dot(
                smat[...], rt, preferred_element_type=F32).astype(BF16).reshape(2, 8, TILE, 256)
            return 0
        lax.fori_loop(0, 4, op_half, 0)
        os_copy(t).start()
        return 0

    lax.fori_loop(0, 4, op_step, 0)

    cp_own_t.wait()

    def t1_wait(i, _):
        p = orb_peer(i)
        rcopy(th.at[c], tbuf.at[j, p], s_t1.at[i], r_t1.at[p], (c, p)).wait_recv()
        return 0

    lax.fori_loop(1, 16, t1_wait, 0)
    jx = (1 - xl) * 4 + y
    cp_tx = rcopy(tbuf.at[j], tbuf.at[j], s_tx, r_tx, xpart)
    cp_tx.start()

    def ty(slot, which, up):
        to = yp if up else ym
        return rcopy(tbuf.at[slot], tbuf.at[slot], s_ty.at[which, int(up)], r_ty.at[which, int(up)],
                     plane(xl * 4 + to))

    ty(j, 0, True).start()
    ty(j, 0, False).start()

    def op_copy(t, i):
        jj = plane_peer(i)
        return rcopy(osum.at[t, jj], opl.at[t, j], s_op.at[t, i], r_op.at[t, j], plane(jj))

    def sum_step(t, _):
        os_copy(t).wait_recv()
        osum[t] = (opart[t, core].astype(F32) + osib[t].astype(F32)).astype(BF16)
        opl[t, j] = osum[t, j]

        def go(i, _):
            op_copy(t, i).start()
            return 0
        lax.fori_loop(1, 8, go, 0)
        return 0

    lax.fori_loop(0, 4, sum_step, 0)

    rcopy(tbuf.at[jx], tbuf.at[jx], s_tx, r_tx, xpart).wait_recv()
    ty(jx, 1, True).start()
    ty(jx, 1, False).start()

    od_copy = lambda t: rcopy(ored.at[t], obuf.at[o, t], s_od.at[t], r_od.at[o, t], (c, dest))

    def red_step(t, _):
        def w(i, _):
            jj = plane_peer(i)
            rcopy(osum.at[t, jj], opl.at[t, jj], s_op.at[t, i], r_op.at[t, jj], plane(jj)).wait_recv()
            return 0
        lax.fori_loop(1, 8, w, 0)
        tot = opl[t, 0].astype(F32)
        for q in range(1, 8):
            tot = tot + opl[t, q].astype(F32)

        @pl.when(o != dest)
        def _():
            ored[t] = tot.astype(BF16)
            od_copy(t).start()

        @pl.when(o == dest)
        def _():
            obuf[o, t] = tot.astype(BF16)
        return 0

    lax.fori_loop(0, 4, red_step, 0)

    def tf(which, up):
        source = ym if up else yp
        slot = (xl if which == 0 else 1 - xl) * 4 + source
        h = 0 if up else 8
        to = yp if up else ym
        piece = tbuf.at[slot, pl.ds(h, 8)]
        return rcopy(piece, piece, s_tf.at[which, int(up)], r_tf.at[which, int(up)], plane(xl * 4 + to))

    for which in (0, 1):
        for up in (True, False):
            slot = (xl if which == 0 else 1 - xl) * 4 + (ym if up else yp)
            rcopy(tbuf.at[slot], tbuf.at[slot], s_ty.at[which, int(up)], r_ty.at[which, int(up)], sib).wait_recv()
            tf(which, up).start()

    def as_copy(p):
        return rcopy(abuf.at[core, p], abuf.at[core, p], s_as.at[p], r_as.at[p], sib)

    cp_own_a.wait()
    as_copy(o).start()

    def a_fwd(i, _):
        p = lax.rem(o - i + 16, 16)
        rcopy(cr.at[pl.ds(4 * p, 4)], abuf.at[core, p], s_a.at[i], r_a.at[p], (c, p)).wait_recv()
        as_copy(p).start()
        return 0

    lax.fori_loop(1, 16, a_fwd, 0)

    @pl.when(o == dest)
    def _():
        cp_phi_own.wait()

        def w(i, _):
            p = orb_peer(i)
            rcopy(phi, pbuf.at[p], s_phi, r_phi.at[p], (c, dest)).wait_recv()

            def wt(t, _):
                rcopy(ored.at[t], obuf.at[p, t], s_od.at[t], r_od.at[p, t], (c, dest)).wait_recv()
                return 0
            lax.fori_loop(0, 4, wt, 0)
            return 0
        lax.fori_loop(1, 16, w, 0)
        term[0] = pbuf[...].reshape(1024, 200)
        acc[...] = pbuf[...].reshape(1024, 200).astype(F32)
        for degree in range(1, ORDER + 1):
            src, dst = (degree - 1) % 2, degree % 2

            def mm(b, _):
                rows = pl.ds(pl.multiple_of(b * 256, 256), 256)
                lhs = obuf[pl.ds(4 * b, 4)].reshape(256, 1024)
                prod = jnp.dot(lhs, term[src], preferred_element_type=F32)
                new = (prod / degree).astype(BF16)
                term[dst, rows] = new
                acc[rows] = acc[rows] + new.astype(F32)
                return 0
            lax.fori_loop(0, 4, mm, 0)
        res[...] = acc[...].astype(BF16).reshape(16, 64, 200)

        def send(i, _):
            p = orb_peer(i)
            rcopy(res.at[p], land, s_w.at[i], r_w, (c, p)).start()
            return 0
        lax.fori_loop(1, 16, send, 0)

    for up in (True, False):
        for which in (0, 1):
            slot = (xl if which == 0 else 1 - xl) * 4 + y2
            piece = tbuf.at[slot, pl.ds(0 if up else 8, 8)]
            rcopy(piece, piece, s_tf.at[which, int(up)], r_tf.at[which, int(up)], sib).wait_recv()

    def as_wait(p, _):
        rcopy(abuf.at[1 - core, p], abuf.at[1 - core, p], s_as.at[p], r_as.at[p], sib).wait_recv()
        return 0

    lax.fori_loop(0, 16, as_wait, 0)

    def tr_step(i, _):
        for h in range(8):
            blk = abuf[i // 4, pl.ds(2 * h, 2), lax.rem(i, 4)].reshape(128, 200)
            a_t[i, :, 128 * h:128 * h + 128] = blk.T
        return 0

    lax.fori_loop(0, 8, tr_step, 0)
    eye = iota((200, 200), 0) == iota((200, 200), 1)

    def w_step(jj, tot):
        b = tbuf[jj].reshape(1024, 200)

        def half(h, _):
            x_buf[pl.ds(4 * h, 4)] = jnp.dot(
                a_t[pl.ds(4 * h, 4)].reshape(800, 1024), b,
                preferred_element_type=F32).astype(BF16).reshape(4, 200, 200)
            return 0
        lax.fori_loop(0, 2, half, 0)

        def sq(i, d):
            xb = x_buf[i]
            return d + jnp.dot(xb, xb, preferred_element_type=F32)
        d = lax.fori_loop(0, 8, sq, jnp.zeros((200, 200), F32))
        value = jnp.sum(jnp.where(eye, d, 0.0))
        return tot + jnp.where(iota((8, 128), 1) == 2 * jj + core, value, 0.0)

    pairs = lax.fori_loop(0, 8, w_step, jnp.zeros((8, 128), F32))

    ebuf[o] = pairs

    def e1(i):
        return rcopy(ebuf.at[o], ebuf.at[o], s_e1.at[i], r_e1.at[o], (c, orb_peer(i)))

    def e1_start(i, _):
        e1(i).start()
        return 0

    lax.fori_loop(1, 16, e1_start, 0)

    def e1_wait(i, _):
        p = orb_peer(i)
        rcopy(ebuf.at[p], ebuf.at[p], s_e1.at[i], r_e1.at[p], (c, p)).wait_recv()
        return 0

    @pl.when(o == dest)
    def _():
        wout[...] = res[o]

    @pl.when(o != dest)
    def _():
        rcopy(land, land, s_w.at[0], r_w, (c, dest)).wait_recv()
        wout[...] = land[...]

    lax.fori_loop(1, 16, e1_wait, 0)
    bias = jnp.where(iota((16, 128), 1) < 64, fb_all, 0.0)
    coulomb = jnp.sum(bias * bias, axis=1, keepdims=True)
    wl = iota((16, 128), 0) == iota((16, 128), 1)
    e_row = jnp.sum(jnp.where(wl, coulomb, 0.0), axis=0, keepdims=True)
    one_row = jnp.sum(jnp.where(wl, fb_all[:, 64:65], 0.0), axis=0, keepdims=True)
    e2buf[c] = e_row - jnp.sum(ebuf[...], axis=0)

    def e2(i):
        return rcopy(e2buf.at[c], e2buf.at[c], s_e2.at[i], r_e2.at[c], (lax.rem(c + i, 16), o))

    def e2_start(i, _):
        e2(i).start()
        return 0

    lax.fori_loop(1, 16, e2_start, 0)

    def e2_wait(i, _):
        p = lax.rem(c + i, 16)
        rcopy(e2buf.at[p], e2buf.at[p], s_e2.at[i], r_e2.at[p], (p, o)).wait_recv()
        return 0

    lax.fori_loop(1, 16, e2_wait, 0)
    en[...] = one_row + 0.5 / VECTORS * jnp.sum(e2buf[...], axis=0)

    def sent(i, _):
        t1(i).wait_send()
        a2a(i).wait_send()
        fb_copy(i).wait_send()
        e1(i).wait_send()
        e2(i).wait_send()
        return 0

    lax.fori_loop(1, 16, sent, 0)

    def sent_as(p, _):
        as_copy(p).wait_send()
        return 0

    lax.fori_loop(0, 16, sent_as, 0)
    cp_tx.wait_send()
    for which in (0, 1):
        for up in (True, False):
            ty(j if which == 0 else jx, which, up).wait_send()
            tf(which, up).wait_send()

    def sent_o(t, _):
        os_copy(t).wait_send()

        def go(i, _):
            op_copy(t, i).wait_send()
            return 0
        lax.fori_loop(1, 8, go, 0)
        return 0

    lax.fori_loop(0, 4, sent_o, 0)

    @pl.when(o != dest)
    def _():
        cp_phi.wait_send()

        def go(t, _):
            od_copy(t).wait_send()
            return 0
        lax.fori_loop(0, 4, go, 0)

    @pl.when(o == dest)
    def _():
        def go(i, _):
            p = orb_peer(i)
            rcopy(res.at[p], land, s_w.at[i], r_w, (c, p)).wait_send()
            return 0
        lax.fori_loop(1, 16, go, 0)


def body(phi_walkers, theta_half, chol_vectors, chol_rotated, hcore_rotated, aux_fields):
    flip = lambda v: jnp.swapaxes(v, -1, -2)
    vm = pl.BlockSpec(memory_space=pltpu.VMEM)
    hbm = pl.BlockSpec(memory_space=pl.ANY)
    dma = pltpu.SemaphoreType.DMA
    sems = [(6,), (16,), (16,), (), (), (2, 2), (2, 2), (2, 2), (2, 2), (), (16,),
            (16,), (16,), (16,), (16,), (16,), (16,), (4,), (4,), (4, 8), (4, 8), (4,), (16, 4),
            (16,), (), (16,), (16,), (16,), (16,)]
    wout, en = pl.pallas_call(
        kernel,
        out_shape=(jax.ShapeDtypeStruct((64, 200), BF16), jax.ShapeDtypeStruct((8, 128), F32)),
        in_specs=[hbm, hbm, hbm, hbm, vm, vm],
        out_specs=(vm, vm),
        scratch_shapes=[
            pltpu.VMEM((64, 64, 200), BF16),
            pltpu.VMEM((64, 64, 1024), BF16),
            pltpu.VMEM((16, 64, 200), BF16),
            pltpu.VMEM((8, 16, 64, 200), BF16),
            pltpu.VMEM((2, 16, 4, 64, 200), BF16),
            pltpu.VMEM((8, 200, 1024), BF16),
            pltpu.VMEM((16, 16, 128), F32),
            pltpu.VMEM((256, 1024), BF16),
            pltpu.VMEM((4, 2, 8, TILE, 1024), BF16),
            pltpu.VMEM((4, 8, TILE, 1024), BF16),
            pltpu.VMEM((4, 8, TILE, 1024), BF16),
            pltpu.VMEM((4, 8, TILE, 1024), BF16),
            pltpu.VMEM((16, 4, TILE, 1024), BF16),
            pltpu.VMEM((4, TILE, 1024), BF16),
            pltpu.VMEM((16, 64, 200), BF16),
            pltpu.VMEM((2, 1024, 200), BF16),
            pltpu.VMEM((1024, 200), F32),
            pltpu.VMEM((16, 64, 200), BF16),
            pltpu.VMEM((64, 200), BF16),
            pltpu.VMEM((8, 200, 200), BF16),
            pltpu.VMEM((16, 8, 128), F32),
            pltpu.VMEM((16, 8, 128), F32),
        ] + [dma(s) if s else dma for s in sems],
        compiler_params=pltpu.CompilerParams(
            collective_id=0, has_side_effects=True, vmem_limit_bytes=56 << 20),
        cost_estimate=pl.CostEstimate(flops=14 * 10**9, bytes_accessed=12 * 10**6, transcendentals=0),
    )(
        flip(phi_walkers)[0],
        flip(theta_half),
        chol_vectors,
        flip(chol_rotated),
        flip(hcore_rotated),
        aux_fields,
    )
    return flip(wout)[None], en[0, :16]


def solution(mesh):
    return jax.shard_map(
        body,
        mesh=mesh,
        in_specs=(
            P("chol", None, "orb"),
            P(None, None, "orb"),
            P("chol", "orb", None),
            P("chol", None, "orb"),
            P(None, "orb"),
            P(None, "chol"),
        ),
        out_specs=(P("chol", None, "orb"), P()),
        check_vma=False,
    )
```

```python
import jax
import jax.numpy as jnp
from jax import lax
from jax.experimental import pallas as pl
from jax.experimental.pallas import tpu as pltpu
from jax.sharding import PartitionSpec as P

ORDER = 4
MESH = pl.DeviceIdType.MESH
F32 = jnp.float32
BF16 = jnp.bfloat16
VECTORS = 1024
TILE = 16


def iota(shape, dim):
    return lax.broadcasted_iota(jnp.int32, shape, dim)


def kernel(phi, th, cv, cr, hc, aux, wout, en,
           crv, cvv, thv, zsum, tbuf, pk, abuf, a_t, fbx, smat, opart, osib, osum, opl, obuf, ored,
           pbuf, term, acc, res, land, x_up, x_lo, ebuf, e2buf,
           s_loc, s_cv, s_t1, r_t1, s_tx, r_tx, s_ty, r_ty, s_tf, r_tf, s_phi, r_phi,
           s_a, r_a, s_as, r_as, s_fb, r_fb, s_os, r_os, s_op, r_op, s_od, r_od,
           s_w, r_w, s_e1, r_e1, s_e2, r_e2):
    c = lax.axis_index("chol")
    o = lax.axis_index("orb")
    core = lax.rem(c, 2)
    xl = c // 8
    y = lax.rem(c // 2, 4)
    j = c // 2
    sib = (2 * j + 1 - core, o)
    yp = lax.rem(y + 1, 4)
    ym = lax.rem(y + 3, 4)
    y2 = lax.rem(y + 2, 4)

    def plane(jj):
        return (2 * jj + core, o)

    xpart = plane((1 - xl) * 4 + y)
    dest = core * 8 + lax.rem(2 * y + xl + 4 * core, 8)

    def rcopy(src, dst, ss, rs, dev):
        return pltpu.make_async_remote_copy(
            src_ref=src, dst_ref=dst, send_sem=ss, recv_sem=rs, device_id=dev, device_id_type=MESH)

    def orb_peer(i):
        return lax.rem(o + i, 16)

    def plane_peer(i):
        return lax.rem(j + i, 8)

    cp_cr = pltpu.make_async_copy(cr, crv, s_loc.at[0])
    cp_cr.start()
    cp_th = pltpu.make_async_copy(th, thv, s_loc.at[1])
    cp_th.start()

    def cv_copy(q):
        return pltpu.make_async_copy(cv.at[pl.ds(8 * q, 8)], cvv.at[pl.ds(8 * q, 8)], s_cv.at[q])

    bar = pltpu.get_barrier_semaphore()

    def sig_orb(i, _):
        pl.semaphore_signal(bar, inc=1, device_id=(c, orb_peer(i)), device_id_type=MESH)
        return 0

    def sig_chol(i, _):
        pl.semaphore_signal(bar, inc=1, device_id=(lax.rem(c + i, 16), o), device_id_type=MESH)
        return 0

    lax.fori_loop(1, 16, sig_orb, 0)
    lax.fori_loop(1, 16, sig_chol, 0)
    pl.semaphore_wait(bar, 30)

    cp_own_t = pltpu.make_async_copy(th.at[c], tbuf.at[j, o], s_loc.at[3])
    cp_own_t.start()

    def z_peer(i):
        return (o // 8) * 8 + lax.rem(o + i, 8)

    def t1(i):
        return rcopy(th.at[c], tbuf.at[j, o], s_t1.at[i], r_t1.at[o], (c, z_peer(i)))

    def t1_start(i, _):
        t1(i).start()
        return 0

    lax.fori_loop(1, 8, t1_start, 0)

    cp_phi = rcopy(phi, pbuf.at[o], s_phi, r_phi.at[o], (c, dest))
    cp_phi_own = pltpu.make_async_copy(phi, pbuf.at[o], s_loc.at[4])

    @pl.when(o != dest)
    def _():
        cp_phi.start()

    @pl.when(o == dest)
    def _():
        cp_phi_own.start()

    def a2a(i):
        p = orb_peer(i)
        return rcopy(pk.at[p], abuf.at[core, o], s_a.at[i], r_a.at[o], (c, p))

    def a2a_start(i, _):
        a2a(i).start()
        return 0

    cp_th.wait()
    cp_cr.wait()

    def cv_start(q, _):
        cv_copy(q).start()
        return 0

    lax.fori_loop(0, 8, cv_start, 0)
    def pack(i, _):
        for v in range(4):
            pk[i, :, 200 * v:200 * v + 200] = crv[4 * i + v]
        pk[i, :, 800:] = jnp.zeros((64, 96), BF16)
        return 0

    lax.fori_loop(0, 16, pack, 0)
    cp_own_a = pltpu.make_async_copy(pk.at[o], abuf.at[core, o], s_loc.at[5])
    cp_own_a.start()

    mask = (iota((64, 512), 0) == lax.rem(iota((64, 512), 1), 64)).astype(F32)

    def fb_step(i, _):
        rhs = crv[pl.ds(8 * i, 8)].reshape(512, 200)
        z = lax.dot_general(thv[...].reshape(1024, 200), rhs, (((1,), (1,)), ((), ())),
                            preferred_element_type=F32)
        zsum[:, pl.ds(pl.multiple_of(512 * i, 512), 512)] = jnp.sum(
            z.reshape(16, 64, 512) * mask[None], axis=1)
        return 0

    lax.fori_loop(0, 4, fb_step, 0)
    cp_own_t.wait()

    def t1x(p):
        return rcopy(tbuf.at[j, p], tbuf.at[j, p], s_t1.at[8 + lax.rem(p, 8)], r_t1.at[p], (c, lax.rem(o + 8, 16)))

    t1x(o).start()

    def t1_wait(i, _):
        p = z_peer(i)
        rcopy(th.at[c], tbuf.at[j, p], s_t1.at[i], r_t1.at[p], (c, p)).wait_recv()
        t1x(p).start()
        return 0

    lax.fori_loop(1, 8, t1_wait, 0)

    lax.fori_loop(4, 8, fb_step, 0)
    z1 = lax.dot_general(thv[...].reshape(1024, 200), hc[...], (((1,), (1,)), ((), ())),
                         preferred_element_type=F32)
    z1 = jnp.sum(z1.reshape(16, 64, 64) * mask[None, :, :64], axis=1)
    one_part = jnp.sum(z1, axis=1, keepdims=True)
    zs = zsum[...]
    hi = zs.astype(BF16)
    lo = (zs - hi.astype(F32)).astype(BF16)
    ind = (iota((4096, 128), 1) == iota((4096, 128), 0) // 64).astype(BF16)
    both = jnp.dot(jnp.concatenate([hi, lo], axis=0), ind, preferred_element_type=F32)
    fbx[o] = (both[:16] + both[16:]
              + jnp.where(iota((16, 128), 1) == 64, one_part, 0.0))

    def fb_copy(i):
        return rcopy(fbx.at[o], fbx.at[o], s_fb.at[i], r_fb.at[o], (c, orb_peer(i)))

    def fb_start(i, _):
        fb_copy(i).start()
        return 0

    lax.fori_loop(1, 16, fb_start, 0)
    lax.fori_loop(1, 16, a2a_start, 0)

    def t1x_wait(i, _):
        t1x(lax.rem(z_peer(i) + 8, 16)).wait_recv()
        return 0

    lax.fori_loop(0, 8, t1x_wait, 0)
    jx = (1 - xl) * 4 + y

    def tx(slot, g):
        piece = tbuf.at[slot, pl.ds(4 * g, 4)]
        return rcopy(piece, piece, s_tx.at[g], r_tx.at[g], xpart)


    def ty(slot, which, up, g):
        to = yp if up else ym
        piece = tbuf.at[slot, pl.ds(4 * g, 4)]
        return rcopy(piece, piece, s_ty.at[which, int(up), g], r_ty.at[which, int(up), g],
                     plane(xl * 4 + to))

    def tx_start(g, _):
        tx(j, g).start()
        ty(j, 0, True, g).start()
        ty(j, 0, False, g).start()
        return 0

    lax.fori_loop(0, 4, tx_start, 0)


    def fb_wait(i, _):
        p = orb_peer(i)
        rcopy(fbx.at[p], fbx.at[p], s_fb.at[i], r_fb.at[p], (c, p)).wait_recv()
        return 0

    lax.fori_loop(1, 16, fb_wait, 0)
    fb_all = jnp.sum(fbx[...], axis=0)
    shifted = (aux[...] - fb_all[:, :64]).astype(BF16)

    row = iota((256, 16), 0)
    ew = (iota((256, 16), 1) == 2 * lax.rem(row // TILE, 8) + row // 128).astype(BF16)
    ea = (iota((64, 1024), 0) == iota((64, 1024), 1) // TILE).astype(BF16)
    spread = jnp.dot(jnp.dot(ew, shifted, preferred_element_type=F32).astype(BF16), ea,
                     preferred_element_type=F32)
    diag = lax.rem(iota((256, 1024), 0), TILE) == lax.rem(iota((256, 1024), 1), TILE)
    smat[...] = jnp.where(diag, spread, 0.0).astype(BF16)

    def cv_wait(q, _):
        cv_copy(q).wait()
        return 0

    lax.fori_loop(0, 8, cv_wait, 0)

    def os_copy(t, q):
        return rcopy(opart.at[t, 1 - core, q], osib.at[t, q], s_os.at[t, q], r_os.at[t, q], sib)

    def op_step(t, _):
        def op_half(h, _):
            cols = pl.ds(pl.multiple_of(h * 256, 256), 256)
            rt = cvv[:, pl.ds(pl.multiple_of(TILE * t, TILE), TILE), cols].reshape(1024, 256)
            opart[t, :, :, :, cols] = jnp.dot(
                smat[...], rt, preferred_element_type=F32).astype(BF16).reshape(2, 8, TILE, 256)
            return 0
        lax.fori_loop(0, 4, op_half, 0)

        def os_start(q, _):
            os_copy(t, q).start()
            return 0
        lax.fori_loop(0, 8, os_start, 0)
        return 0

    lax.fori_loop(0, 4, op_step, 0)

    def ty_start(g, _):
        tx(jx, g).wait_recv()
        ty(jx, 1, True, g).start()
        ty(jx, 1, False, g).start()
        return 0

    lax.fori_loop(0, 4, ty_start, 0)

    def op_copy(t, i):
        jj = plane_peer(i)
        return rcopy(osum.at[t, jj], opl.at[t, j], s_op.at[t, i], r_op.at[t, j], plane(jj))

    def sum_step(t, _):
        def os_wait(q, _):
            os_copy(t, q).wait_recv()
            return 0
        lax.fori_loop(0, 8, os_wait, 0)
        osum[t] = (opart[t, core].astype(F32) + osib[t].astype(F32)).astype(BF16)
        opl[t, j] = osum[t, j]

        def go(i, _):
            op_copy(t, i).start()
            return 0
        lax.fori_loop(1, 8, go, 0)
        return 0

    lax.fori_loop(0, 4, sum_step, 0)
    def tf_slot(which, up):
        return (xl if which == 0 else 1 - xl) * 4 + (ym if up else yp)

    def tf(which, up, g):
        piece = tbuf.at[tf_slot(which, up), pl.ds(4 * g + (0 if up else 8), 4)]
        return rcopy(piece, piece, s_tf.at[which, int(up), g], r_tf.at[which, int(up), g],
                     plane(xl * 4 + (yp if up else ym)))

    def tf_step(which):
        def step(g, _):
            for up in (True, False):
                ty(tf_slot(which, up), which, up, g + (0 if up else 2)).wait_recv()
                tf(which, up, g).start()
            return 0
        lax.fori_loop(0, 2, step, 0)

    tf_step(0)

    od_copy = lambda t: rcopy(ored.at[t], obuf.at[o, t], s_od.at[t], r_od.at[o, t], (c, dest))

    def red_step(t, _):
        def w(i, _):
            jj = plane_peer(i)
            rcopy(osum.at[t, jj], opl.at[t, jj], s_op.at[t, i], r_op.at[t, jj], plane(jj)).wait_recv()
            return 0
        lax.fori_loop(1, 8, w, 0)
        tot = opl[t, 0].astype(F32)
        for q in range(1, 8):
            tot = tot + opl[t, q].astype(F32)

        @pl.when(o != dest)
        def _():
            ored[t] = tot.astype(BF16)
            od_copy(t).start()

        @pl.when(o == dest)
        def _():
            obuf[o, t] = tot.astype(BF16)
        return 0

    lax.fori_loop(0, 4, red_step, 0)

    tf_step(1)

    def as_copy(p):
        return rcopy(abuf.at[core, p], abuf.at[core, p], s_as.at[p], r_as.at[p], sib)

    cp_own_a.wait()
    as_copy(o).start()

    def a_fwd(i, _):
        p = lax.rem(o - i + 16, 16)
        rcopy(pk.at[p], abuf.at[core, p], s_a.at[i], r_a.at[p], (c, p)).wait_recv()
        as_copy(p).start()
        return 0

    lax.fori_loop(1, 16, a_fwd, 0)

    def as_wait(p, _):
        rcopy(abuf.at[1 - core, p], abuf.at[1 - core, p], s_as.at[p], r_as.at[p], sib).wait_recv()
        return 0

    lax.fori_loop(0, 16, as_wait, 0)

    def tr_step(i, _):
        cols = pl.ds(pl.multiple_of(128 * i, 128), 128)
        for k in range(2):
            blk = abuf[k, pl.ds(2 * i, 2)].reshape(128, 896)
            a_t[k, :, cols] = blk.T[:800]
        return 0

    lax.fori_loop(0, 8, tr_step, 0)
    x_lo[...] = jnp.zeros_like(x_lo)
    x_up[...] = jnp.zeros_like(x_up)
    eye = iota((200, 200), 0) == iota((200, 200), 1)

    def w_step(r, tot):
        q = r // 2
        jj = lax.rem(xl + r, 2) * 4 + lax.rem(y + q + (q // 2) * (5 - 2 * q), 4)
        b = tbuf[jj].reshape(1024, 200)

        def half(h, _):
            x = jnp.dot(a_t[h], b,
                        preferred_element_type=F32).astype(BF16).reshape(4, 200, 200)
            for q in range(4):
                x_up[4 * h + q, :200, :] = x[q]
                x_lo[:, pl.ds(pl.multiple_of(1024 * h, 256) + 256 * q, 200)] = x[q]
            return 0
        lax.fori_loop(0, 2, half, 0)
        d = jnp.dot(x_lo[...], x_up[...].reshape(2048, 200), preferred_element_type=F32)
        value = jnp.sum(jnp.where(eye, d, 0.0))
        return tot + jnp.where(iota((8, 128), 1) == 2 * jj + core, value, 0.0)

    pairs = lax.fori_loop(0, 2, w_step, jnp.zeros((8, 128), F32))

    @pl.when(o == dest)
    def _():
        cp_phi_own.wait()

        def w(i, _):
            p = orb_peer(i)
            rcopy(phi, pbuf.at[p], s_phi, r_phi.at[p], (c, dest)).wait_recv()

            def wt(t, _):
                rcopy(ored.at[t], obuf.at[p, t], s_od.at[t], r_od.at[p, t], (c, dest)).wait_recv()
                return 0
            lax.fori_loop(0, 4, wt, 0)
            return 0
        lax.fori_loop(1, 16, w, 0)
        term[0] = pbuf[...].reshape(1024, 200)
        acc[...] = pbuf[...].reshape(1024, 200).astype(F32)
        for degree in range(1, ORDER + 1):
            src, dst = (degree - 1) % 2, degree % 2

            def mm(b, _):
                rows = pl.ds(pl.multiple_of(b * 256, 256), 256)
                lhs = obuf[pl.ds(4 * b, 4)].reshape(256, 1024)
                prod = jnp.dot(lhs, term[src], preferred_element_type=F32)
                new = (prod / degree).astype(BF16)
                term[dst, rows] = new
                acc[rows] = acc[rows] + new.astype(F32)
                return 0
            lax.fori_loop(0, 4, mm, 0)
        res[...] = acc[...].astype(BF16).reshape(16, 64, 200)

        def send(i, _):
            p = orb_peer(i)
            rcopy(res.at[p], land, s_w.at[i], r_w, (c, p)).start()
            return 0
        lax.fori_loop(1, 16, send, 0)

    def ty_rest(g, _):
        for which in (0, 1):
            for up in (True, False):
                ty(tf_slot(which, up), which, up, g + (2 if up else 0)).wait_recv()
        return 0

    lax.fori_loop(0, 2, ty_rest, 0)

    pairs = lax.fori_loop(2, 6, w_step, pairs)

    def tf_wait(g, _):
        for which in (0, 1):
            for up in (True, False):
                slot = (xl if which == 0 else 1 - xl) * 4 + y2
                piece = tbuf.at[slot, pl.ds(4 * g + (0 if up else 8), 4)]
                rcopy(piece, piece, s_tf.at[which, int(up), g], r_tf.at[which, int(up), g], sib).wait_recv()
        return 0

    lax.fori_loop(0, 2, tf_wait, 0)

    pairs = lax.fori_loop(6, 8, w_step, pairs)

    ebuf[o] = pairs

    def e1(i):
        return rcopy(ebuf.at[o], ebuf.at[o], s_e1.at[i], r_e1.at[o], (c, orb_peer(i)))

    def e1_start(i, _):
        e1(i).start()
        return 0

    lax.fori_loop(1, 16, e1_start, 0)

    def e1_wait(i, _):
        p = orb_peer(i)
        rcopy(ebuf.at[p], ebuf.at[p], s_e1.at[i], r_e1.at[p], (c, p)).wait_recv()
        return 0

    @pl.when(o == dest)
    def _():
        wout[...] = res[o]

    @pl.when(o != dest)
    def _():
        rcopy(land, land, s_w.at[0], r_w, (c, dest)).wait_recv()
        wout[...] = land[...]

    lax.fori_loop(1, 16, e1_wait, 0)
    bias = jnp.where(iota((16, 128), 1) < 64, fb_all, 0.0)
    coulomb = jnp.sum(bias * bias, axis=1, keepdims=True)
    wl = iota((16, 128), 0) == iota((16, 128), 1)
    e_row = jnp.sum(jnp.where(wl, coulomb, 0.0), axis=0, keepdims=True)
    one_row = jnp.sum(jnp.where(wl, fb_all[:, 64:65], 0.0), axis=0, keepdims=True)
    e2buf[c] = e_row - jnp.sum(ebuf[...], axis=0)

    def e2(i):
        return rcopy(e2buf.at[c], e2buf.at[c], s_e2.at[i], r_e2.at[c], (lax.rem(c + i, 16), o))

    def e2_start(i, _):
        e2(i).start()
        return 0

    lax.fori_loop(1, 16, e2_start, 0)

    def e2_wait(i, _):
        p = lax.rem(c + i, 16)
        rcopy(e2buf.at[p], e2buf.at[p], s_e2.at[i], r_e2.at[p], (p, o)).wait_recv()
        return 0

    lax.fori_loop(1, 16, e2_wait, 0)
    en[...] = (one_row + 0.5 / VECTORS * jnp.sum(e2buf[...], axis=0))[0, :16]

    def sent(i, _):
        a2a(i).wait_send()
        fb_copy(i).wait_send()
        e1(i).wait_send()
        e2(i).wait_send()
        return 0

    lax.fori_loop(1, 16, sent, 0)

    def sent_t1(i, _):
        t1(i).wait_send()
        return 0

    lax.fori_loop(1, 8, sent_t1, 0)

    def sent_t1x(i, _):
        t1x(z_peer(i)).wait_send()
        return 0

    lax.fori_loop(0, 8, sent_t1x, 0)

    def sent_as(p, _):
        as_copy(p).wait_send()
        return 0

    lax.fori_loop(0, 16, sent_as, 0)
    def sent_th(g, _):
        tx(j, g).wait_send()
        for up in (True, False):
            ty(j, 0, up, g).wait_send()
            ty(jx, 1, up, g).wait_send()
        return 0

    lax.fori_loop(0, 4, sent_th, 0)

    def sent_tf(g, _):
        for which in (0, 1):
            for up in (True, False):
                tf(which, up, g).wait_send()
        return 0

    lax.fori_loop(0, 2, sent_tf, 0)

    def sent_o(t, _):
        def so(q, _):
            os_copy(t, q).wait_send()
            return 0
        lax.fori_loop(0, 8, so, 0)

        def go(i, _):
            op_copy(t, i).wait_send()
            return 0
        lax.fori_loop(1, 8, go, 0)
        return 0

    lax.fori_loop(0, 4, sent_o, 0)

    @pl.when(o != dest)
    def _():
        cp_phi.wait_send()

        def go(t, _):
            od_copy(t).wait_send()
            return 0
        lax.fori_loop(0, 4, go, 0)

    @pl.when(o == dest)
    def _():
        def go(i, _):
            p = orb_peer(i)
            rcopy(res.at[p], land, s_w.at[i], r_w, (c, p)).wait_send()
            return 0
        lax.fori_loop(1, 16, go, 0)


def body(phi_walkers, theta_half, chol_vectors, chol_rotated, hcore_rotated, aux_fields):
    flip = lambda v: jnp.swapaxes(v, -1, -2)
    vm = pl.BlockSpec(memory_space=pltpu.VMEM)
    hbm = pl.BlockSpec(memory_space=pl.ANY)
    dma = pltpu.SemaphoreType.DMA
    sems = [(6,), (8,), (16,), (16,), (4,), (4,), (2, 2, 4), (2, 2, 4), (2, 2, 2), (2, 2, 2), (), (16,),
            (16,), (16,), (16,), (16,), (16,), (16,), (4, 8), (4, 8), (4, 8), (4, 8), (4,), (16, 4),
            (16,), (), (16,), (16,), (16,), (16,)]
    wout, en = pl.pallas_call(
        kernel,
        out_shape=(jax.ShapeDtypeStruct((64, 200), BF16), jax.ShapeDtypeStruct((16,), F32)),
        in_specs=[hbm, hbm, hbm, hbm, vm, vm],
        out_specs=(vm, vm),
        scratch_shapes=[
            pltpu.VMEM((64, 64, 200), BF16),
            pltpu.VMEM((64, 64, 1024), BF16),
            pltpu.VMEM((16, 64, 200), BF16),
            pltpu.VMEM((16, 4096), F32),
            pltpu.VMEM((8, 16, 64, 200), BF16),
            pltpu.VMEM((16, 64, 896), BF16),
            pltpu.VMEM((2, 16, 64, 896), BF16),
            pltpu.VMEM((2, 800, 1024), BF16),
            pltpu.VMEM((16, 16, 128), F32),
            pltpu.VMEM((256, 1024), BF16),
            pltpu.VMEM((4, 2, 8, TILE, 1024), BF16),
            pltpu.VMEM((4, 8, TILE, 1024), BF16),
            pltpu.VMEM((4, 8, TILE, 1024), BF16),
            pltpu.VMEM((4, 8, TILE, 1024), BF16),
            pltpu.VMEM((16, 4, TILE, 1024), BF16),
            pltpu.VMEM((4, TILE, 1024), BF16),
            pltpu.VMEM((16, 64, 200), BF16),
            pltpu.VMEM((2, 1024, 200), BF16),
            pltpu.VMEM((1024, 200), F32),
            pltpu.VMEM((16, 64, 200), BF16),
            pltpu.VMEM((64, 200), BF16),
            pltpu.VMEM((8, 256, 200), BF16),
            pltpu.VMEM((200, 2048), BF16),
            pltpu.VMEM((16, 8, 128), F32),
            pltpu.VMEM((16, 8, 128), F32),
        ] + [dma(s) if s else dma for s in sems],
        compiler_params=pltpu.CompilerParams(
            collective_id=0, has_side_effects=True, vmem_limit_bytes=56 << 20),
        cost_estimate=pl.CostEstimate(flops=14 * 10**9, bytes_accessed=12 * 10**6, transcendentals=0),
    )(
        flip(phi_walkers)[0],
        flip(theta_half),
        chol_vectors,
        flip(chol_rotated),
        flip(hcore_rotated),
        aux_fields,
    )
    return flip(wout)[None], en


def solution(mesh):
    return jax.shard_map(
        body,
        mesh=mesh,
        in_specs=(
            P("chol", None, "orb"),
            P(None, None, "orb"),
            P("chol", "orb", None),
            P("chol", None, "orb"),
            P(None, "orb"),
            P(None, "chol"),
        ),
        out_specs=(P("chol", None, "orb"), P()),
        check_vma=False,
    )
```

```python
import jax
import jax.numpy as jnp
from jax import lax
from jax.experimental import pallas as pl
from jax.experimental.pallas import tpu as pltpu
from jax.sharding import PartitionSpec as P

ORDER = 4
MESH = pl.DeviceIdType.MESH
F32 = jnp.float32
BF16 = jnp.bfloat16
VECTORS = 1024
TILE = 16


def iota(shape, dim):
    return lax.broadcasted_iota(jnp.int32, shape, dim)


def kernel(phi, th, cv, cr, hc, aux, wout, en,
           crv, cvv, thv, zsum, tbuf, pk, abuf, a_t, fbx, smat, opart, osib, osum, opl, obuf, ored,
           pbuf, term, acc, res, land, x_up, x_lo, ebuf, e2buf,
           s_loc, s_cv, s_t1, r_t1, s_tx, r_tx, s_ty, r_ty, s_tf, r_tf, s_phi, r_phi,
           s_a, r_a, s_as, r_as, s_fb, r_fb, s_os, r_os, s_op, r_op, s_od, r_od,
           s_w, r_w, s_e1, r_e1, s_e2, r_e2):
    c = lax.axis_index("chol")
    o = lax.axis_index("orb")
    core = lax.rem(c, 2)
    xl = c // 8
    y = lax.rem(c // 2, 4)
    j = c // 2
    sib = (2 * j + 1 - core, o)
    yp = lax.rem(y + 1, 4)
    ym = lax.rem(y + 3, 4)
    y2 = lax.rem(y + 2, 4)

    def plane(jj):
        return (2 * jj + core, o)

    xpart = plane((1 - xl) * 4 + y)
    dest = core * 8 + lax.rem(2 * y + xl + 4 * core, 8)

    def rcopy(src, dst, ss, rs, dev):
        return pltpu.make_async_remote_copy(
            src_ref=src, dst_ref=dst, send_sem=ss, recv_sem=rs, device_id=dev, device_id_type=MESH)

    def orb_peer(i):
        return lax.rem(o + i, 16)

    def plane_peer(i):
        return lax.rem(j + i, 8)

    cp_cr = pltpu.make_async_copy(cr, crv, s_loc.at[0])
    cp_cr.start()
    cp_th = pltpu.make_async_copy(th, thv, s_loc.at[1])
    cp_th.start()

    def cv_copy(q):
        return pltpu.make_async_copy(cv.at[pl.ds(8 * q, 8)], cvv.at[pl.ds(8 * q, 8)], s_cv.at[q])

    bar = pltpu.get_barrier_semaphore()

    def sig_orb(i, _):
        pl.semaphore_signal(bar, inc=1, device_id=(c, orb_peer(i)), device_id_type=MESH)
        return 0

    def sig_chol(i, _):
        pl.semaphore_signal(bar, inc=1, device_id=(lax.rem(c + i, 16), o), device_id_type=MESH)
        return 0

    lax.fori_loop(1, 16, sig_orb, 0)
    lax.fori_loop(1, 16, sig_chol, 0)
    pl.semaphore_wait(bar, 30)

    cp_own_t = pltpu.make_async_copy(th.at[c], tbuf.at[j, o], s_loc.at[3])
    cp_own_t.start()

    def z_peer(i):
        return (o // 8) * 8 + lax.rem(o + i, 8)

    def t1(i):
        return rcopy(th.at[c], tbuf.at[j, o], s_t1.at[i], r_t1.at[o], (c, z_peer(i)))

    def t1_start(i, _):
        t1(i).start()
        return 0

    lax.fori_loop(1, 8, t1_start, 0)

    cp_phi = rcopy(phi, pbuf.at[o], s_phi, r_phi.at[o], (c, dest))
    cp_phi_own = pltpu.make_async_copy(phi, pbuf.at[o], s_loc.at[4])

    @pl.when(o != dest)
    def _():
        cp_phi.start()

    @pl.when(o == dest)
    def _():
        cp_phi_own.start()

    def a2a(i):
        p = orb_peer(i)
        return rcopy(pk.at[p], abuf.at[core, o], s_a.at[i], r_a.at[o], (c, p))

    def a2a_start(i, _):
        a2a(i).start()
        return 0

    cp_th.wait()
    cp_cr.wait()

    def cv_start(q, _):
        cv_copy(q).start()
        return 0

    lax.fori_loop(0, 8, cv_start, 0)
    def pack(i, _):
        for v in range(4):
            pk[i, :, 200 * v:200 * v + 200] = crv[4 * i + v]
        pk[i, :, 800:] = jnp.zeros((64, 96), BF16)
        return 0

    lax.fori_loop(0, 16, pack, 0)
    cp_own_a = pltpu.make_async_copy(pk.at[o], abuf.at[core, o], s_loc.at[5])
    cp_own_a.start()

    mask = (iota((64, 512), 0) == lax.rem(iota((64, 512), 1), 64)).astype(F32)

    def fb_step(i, _):
        rhs = crv[pl.ds(8 * i, 8)].reshape(512, 200)
        z = lax.dot_general(thv[...].reshape(1024, 200), rhs, (((1,), (1,)), ((), ())),
                            preferred_element_type=F32)
        zsum[:, pl.ds(pl.multiple_of(512 * i, 512), 512)] = jnp.sum(
            z.reshape(16, 64, 512) * mask[None], axis=1)
        return 0

    lax.fori_loop(0, 4, fb_step, 0)
    cp_own_t.wait()

    def t1x(p):
        return rcopy(tbuf.at[j, p], tbuf.at[j, p], s_t1.at[8 + lax.rem(p, 8)], r_t1.at[p], (c, lax.rem(o + 8, 16)))

    t1x(o).start()

    def t1_wait(i, _):
        p = z_peer(i)
        rcopy(th.at[c], tbuf.at[j, p], s_t1.at[i], r_t1.at[p], (c, p)).wait_recv()
        t1x(p).start()
        return 0

    lax.fori_loop(1, 8, t1_wait, 0)

    lax.fori_loop(4, 8, fb_step, 0)
    z1 = lax.dot_general(thv[...].reshape(1024, 200), hc[...], (((1,), (1,)), ((), ())),
                         preferred_element_type=F32)
    z1 = jnp.sum(z1.reshape(16, 64, 64) * mask[None, :, :64], axis=1)
    one_part = jnp.sum(z1, axis=1, keepdims=True)
    zs = zsum[...]
    hi = zs.astype(BF16)
    lo = (zs - hi.astype(F32)).astype(BF16)
    ind = (iota((4096, 128), 1) == iota((4096, 128), 0) // 64).astype(BF16)
    both = jnp.dot(jnp.concatenate([hi, lo], axis=0), ind, preferred_element_type=F32)
    fbx[o] = (both[:16] + both[16:]
              + jnp.where(iota((16, 128), 1) == 64, one_part, 0.0))

    def fb_copy(i):
        return rcopy(fbx.at[o], fbx.at[o], s_fb.at[i], r_fb.at[o], (c, orb_peer(i)))

    def fb_start(i, _):
        fb_copy(i).start()
        return 0

    lax.fori_loop(1, 16, fb_start, 0)
    lax.fori_loop(1, 16, a2a_start, 0)

    def t1x_wait(i, _):
        t1x(lax.rem(z_peer(i) + 8, 16)).wait_recv()
        return 0

    lax.fori_loop(0, 8, t1x_wait, 0)
    jx = (1 - xl) * 4 + y

    def tx(slot, g):
        piece = tbuf.at[slot, pl.ds(4 * g, 4)]
        return rcopy(piece, piece, s_tx.at[g], r_tx.at[g], xpart)


    def ty(slot, which, up, g):
        to = yp if up else ym
        piece = tbuf.at[slot, pl.ds(4 * g, 4)]
        return rcopy(piece, piece, s_ty.at[which, int(up), g], r_ty.at[which, int(up), g],
                     plane(xl * 4 + to))

    def tx_start(g, _):
        tx(j, g).start()
        ty(j, 0, True, g).start()
        ty(j, 0, False, g).start()
        return 0

    lax.fori_loop(0, 4, tx_start, 0)


    def fb_wait(i, _):
        p = orb_peer(i)
        rcopy(fbx.at[p], fbx.at[p], s_fb.at[i], r_fb.at[p], (c, p)).wait_recv()
        return 0

    lax.fori_loop(1, 16, fb_wait, 0)
    fb_all = jnp.sum(fbx[...], axis=0)
    shifted = (aux[...] - fb_all[:, :64]).astype(BF16)

    row = iota((256, 16), 0)
    ew = (iota((256, 16), 1) == 2 * lax.rem(row // TILE, 8) + row // 128).astype(BF16)
    ea = (iota((64, 1024), 0) == iota((64, 1024), 1) // TILE).astype(BF16)
    spread = jnp.dot(jnp.dot(ew, shifted, preferred_element_type=F32).astype(BF16), ea,
                     preferred_element_type=F32)
    diag = lax.rem(iota((256, 1024), 0), TILE) == lax.rem(iota((256, 1024), 1), TILE)
    smat[...] = jnp.where(diag, spread, 0.0).astype(BF16)

    def cv_wait(q, _):
        cv_copy(q).wait()
        return 0

    lax.fori_loop(0, 8, cv_wait, 0)

    def os_copy(t, q):
        return rcopy(opart.at[t, 1 - core, q], osib.at[t, q], s_os.at[t, q], r_os.at[t, q], sib)

    def op_step(t, _):
        def op_half(h, _):
            cols = pl.ds(pl.multiple_of(h * 256, 256), 256)
            rt = cvv[:, pl.ds(pl.multiple_of(TILE * t, TILE), TILE), cols].reshape(1024, 256)
            opart[t, :, :, :, cols] = jnp.dot(
                smat[...], rt, preferred_element_type=F32).astype(BF16).reshape(2, 8, TILE, 256)
            return 0
        lax.fori_loop(0, 4, op_half, 0)

        def os_start(q, _):
            os_copy(t, q).start()
            return 0
        lax.fori_loop(0, 8, os_start, 0)
        return 0

    lax.fori_loop(0, 4, op_step, 0)

    def ty_start(g, _):
        tx(jx, g).wait_recv()
        ty(jx, 1, True, g).start()
        ty(jx, 1, False, g).start()
        return 0

    lax.fori_loop(0, 4, ty_start, 0)

    def op_copy(t, i):
        jj = plane_peer(i)
        return rcopy(osum.at[t, jj], opl.at[t, j], s_op.at[t, i], r_op.at[t, j], plane(jj))

    def sum_step(t, _):
        def os_wait(q, _):
            os_copy(t, q).wait_recv()
            return 0
        lax.fori_loop(0, 8, os_wait, 0)
        osum[t] = (opart[t, core].astype(F32) + osib[t].astype(F32)).astype(BF16)
        opl[t, j] = osum[t, j]

        def go(i, _):
            op_copy(t, i).start()
            return 0
        lax.fori_loop(1, 8, go, 0)
        return 0

    lax.fori_loop(0, 4, sum_step, 0)
    def tf_slot(which, up):
        return (xl if which == 0 else 1 - xl) * 4 + (ym if up else yp)

    def tf(which, up, g):
        piece = tbuf.at[tf_slot(which, up), pl.ds(4 * g + (0 if up else 8), 4)]
        return rcopy(piece, piece, s_tf.at[which, int(up), g], r_tf.at[which, int(up), g],
                     plane(xl * 4 + (yp if up else ym)))

    def tf_step(which):
        def step(g, _):
            for up in (True, False):
                ty(tf_slot(which, up), which, up, g + (0 if up else 2)).wait_recv()
                tf(which, up, g).start()
            return 0
        lax.fori_loop(0, 2, step, 0)

    tf_step(0)

    od_copy = lambda t: rcopy(ored.at[t], obuf.at[o, t], s_od.at[t], r_od.at[o, t], (c, dest))

    def red_step(t, _):
        def w(i, _):
            jj = plane_peer(i)
            rcopy(osum.at[t, jj], opl.at[t, jj], s_op.at[t, i], r_op.at[t, jj], plane(jj)).wait_recv()
            return 0
        lax.fori_loop(1, 8, w, 0)
        tot = opl[t, 0].astype(F32)
        for q in range(1, 8):
            tot = tot + opl[t, q].astype(F32)

        @pl.when(o != dest)
        def _():
            ored[t] = tot.astype(BF16)
            od_copy(t).start()

        @pl.when(o == dest)
        def _():
            obuf[o, t] = tot.astype(BF16)
        return 0

    lax.fori_loop(0, 4, red_step, 0)

    tf_step(1)

    def as_copy(p):
        return rcopy(abuf.at[core, p], abuf.at[core, p], s_as.at[p], r_as.at[p], sib)

    cp_own_a.wait()
    as_copy(o).start()

    def a_fwd(i, _):
        p = lax.rem(o - i + 16, 16)
        rcopy(pk.at[p], abuf.at[core, p], s_a.at[i], r_a.at[p], (c, p)).wait_recv()
        as_copy(p).start()
        return 0

    lax.fori_loop(1, 16, a_fwd, 0)

    def as_wait(p, _):
        rcopy(abuf.at[1 - core, p], abuf.at[1 - core, p], s_as.at[p], r_as.at[p], sib).wait_recv()
        return 0

    lax.fori_loop(0, 16, as_wait, 0)

    def tr_step(i, _):
        cols = pl.ds(pl.multiple_of(128 * i, 128), 128)
        for k in range(2):
            blk = abuf[k, pl.ds(2 * i, 2)].reshape(128, 896)
            a_t[k, :, cols] = blk.T[:800]
        return 0

    lax.fori_loop(0, 8, tr_step, 0)
    x_lo[...] = jnp.zeros_like(x_lo)
    x_up[...] = jnp.zeros_like(x_up)
    eye = iota((200, 200), 0) == iota((200, 200), 1)

    def w_step(r, tot):
        q = r // 2
        jj = lax.rem(xl + r, 2) * 4 + lax.rem(y + q + (q // 2) * (5 - 2 * q), 4)
        b = tbuf[jj].reshape(1024, 200)

        def half(h, _):
            x = jnp.dot(a_t[h], b,
                        preferred_element_type=F32).astype(BF16).reshape(4, 200, 200)
            for q in range(4):
                x_up[4 * h + q, :200, :] = x[q]
                x_lo[:, pl.ds(pl.multiple_of(1024 * h, 256) + 256 * q, 200)] = x[q]
            return 0
        lax.fori_loop(0, 2, half, 0)
        d = jnp.dot(x_lo[...], x_up[...].reshape(2048, 200), preferred_element_type=F32)
        value = jnp.sum(jnp.where(eye, d, 0.0))
        return tot + jnp.where(iota((8, 128), 1) == 2 * jj + core, value, 0.0)

    pairs = lax.fori_loop(0, 2, w_step, jnp.zeros((8, 128), F32))

    def ty_rest(g, _):
        for which in (0, 1):
            for up in (True, False):
                ty(tf_slot(which, up), which, up, g + (2 if up else 0)).wait_recv()
        return 0

    lax.fori_loop(0, 2, ty_rest, 0)

    pairs = lax.fori_loop(2, 6, w_step, pairs)

    @pl.when(o == dest)
    def _():
        cp_phi_own.wait()

        def w(i, _):
            p = orb_peer(i)
            rcopy(phi, pbuf.at[p], s_phi, r_phi.at[p], (c, dest)).wait_recv()

            def wt(t, _):
                rcopy(ored.at[t], obuf.at[p, t], s_od.at[t], r_od.at[p, t], (c, dest)).wait_recv()
                return 0
            lax.fori_loop(0, 4, wt, 0)
            return 0
        lax.fori_loop(1, 16, w, 0)
        term[0] = pbuf[...].reshape(1024, 200)
        acc[...] = pbuf[...].reshape(1024, 200).astype(F32)
        for degree in range(1, ORDER + 1):
            src, dst = (degree - 1) % 2, degree % 2

            def mm(b, _):
                rows = pl.ds(pl.multiple_of(b * 512, 512), 512)
                lhs = obuf[pl.ds(8 * b, 8)].reshape(512, 1024)
                prod = jnp.dot(lhs, term[src], preferred_element_type=F32)
                new = (prod * (1.0 / degree)).astype(BF16)
                term[dst, rows] = new
                acc[rows] = acc[rows] + new.astype(F32)
                return 0
            lax.fori_loop(0, 2, mm, 0)
        res[...] = acc[...].astype(BF16).reshape(16, 64, 200)

        def send(i, _):
            p = orb_peer(i)
            rcopy(res.at[p], land, s_w.at[i], r_w, (c, p)).start()
            return 0
        lax.fori_loop(1, 16, send, 0)


    def tf_wait(g, _):
        for which in (0, 1):
            for up in (True, False):
                slot = (xl if which == 0 else 1 - xl) * 4 + y2
                piece = tbuf.at[slot, pl.ds(4 * g + (0 if up else 8), 4)]
                rcopy(piece, piece, s_tf.at[which, int(up), g], r_tf.at[which, int(up), g], sib).wait_recv()
        return 0

    lax.fori_loop(0, 2, tf_wait, 0)

    pairs = lax.fori_loop(6, 8, w_step, pairs)

    ebuf[o] = pairs

    def e1(i):
        return rcopy(ebuf.at[o], ebuf.at[o], s_e1.at[i], r_e1.at[o], (c, orb_peer(i)))

    def e1_start(i, _):
        e1(i).start()
        return 0

    lax.fori_loop(1, 16, e1_start, 0)

    def e1_wait(i, _):
        p = orb_peer(i)
        rcopy(ebuf.at[p], ebuf.at[p], s_e1.at[i], r_e1.at[p], (c, p)).wait_recv()
        return 0

    @pl.when(o == dest)
    def _():
        wout[...] = res[o]

    @pl.when(o != dest)
    def _():
        rcopy(land, land, s_w.at[0], r_w, (c, dest)).wait_recv()
        wout[...] = land[...]

    lax.fori_loop(1, 16, e1_wait, 0)
    bias = jnp.where(iota((16, 128), 1) < 64, fb_all, 0.0)
    coulomb = jnp.sum(bias * bias, axis=1, keepdims=True)
    wl = iota((16, 128), 0) == iota((16, 128), 1)
    e_row = jnp.sum(jnp.where(wl, coulomb, 0.0), axis=0, keepdims=True)
    one_row = jnp.sum(jnp.where(wl, fb_all[:, 64:65], 0.0), axis=0, keepdims=True)
    e2buf[c] = e_row - jnp.sum(ebuf[...], axis=0)

    def e2(i):
        return rcopy(e2buf.at[c], e2buf.at[c], s_e2.at[i], r_e2.at[c], (lax.rem(c + i, 16), o))

    def e2_start(i, _):
        e2(i).start()
        return 0

    lax.fori_loop(1, 16, e2_start, 0)

    def e2_wait(i, _):
        p = lax.rem(c + i, 16)
        rcopy(e2buf.at[p], e2buf.at[p], s_e2.at[i], r_e2.at[p], (p, o)).wait_recv()
        return 0

    lax.fori_loop(1, 16, e2_wait, 0)
    en[...] = (one_row + 0.5 / VECTORS * jnp.sum(e2buf[...], axis=0))[0, :16]

    def sent(i, _):
        a2a(i).wait_send()
        fb_copy(i).wait_send()
        e1(i).wait_send()
        e2(i).wait_send()
        return 0

    lax.fori_loop(1, 16, sent, 0)

    def sent_t1(i, _):
        t1(i).wait_send()
        return 0

    lax.fori_loop(1, 8, sent_t1, 0)

    def sent_t1x(i, _):
        t1x(z_peer(i)).wait_send()
        return 0

    lax.fori_loop(0, 8, sent_t1x, 0)

    def sent_as(p, _):
        as_copy(p).wait_send()
        return 0

    lax.fori_loop(0, 16, sent_as, 0)
    def sent_th(g, _):
        tx(j, g).wait_send()
        for up in (True, False):
            ty(j, 0, up, g).wait_send()
            ty(jx, 1, up, g).wait_send()
        return 0

    lax.fori_loop(0, 4, sent_th, 0)

    def sent_tf(g, _):
        for which in (0, 1):
            for up in (True, False):
                tf(which, up, g).wait_send()
        return 0

    lax.fori_loop(0, 2, sent_tf, 0)

    def sent_o(t, _):
        def so(q, _):
            os_copy(t, q).wait_send()
            return 0
        lax.fori_loop(0, 8, so, 0)

        def go(i, _):
            op_copy(t, i).wait_send()
            return 0
        lax.fori_loop(1, 8, go, 0)
        return 0

    lax.fori_loop(0, 4, sent_o, 0)

    @pl.when(o != dest)
    def _():
        cp_phi.wait_send()

        def go(t, _):
            od_copy(t).wait_send()
            return 0
        lax.fori_loop(0, 4, go, 0)

    @pl.when(o == dest)
    def _():
        def go(i, _):
            p = orb_peer(i)
            rcopy(res.at[p], land, s_w.at[i], r_w, (c, p)).wait_send()
            return 0
        lax.fori_loop(1, 16, go, 0)


def body(phi_walkers, theta_half, chol_vectors, chol_rotated, hcore_rotated, aux_fields):
    flip = lambda v: jnp.swapaxes(v, -1, -2)
    vm = pl.BlockSpec(memory_space=pltpu.VMEM)
    hbm = pl.BlockSpec(memory_space=pl.ANY)
    dma = pltpu.SemaphoreType.DMA
    sems = [(6,), (8,), (16,), (16,), (4,), (4,), (2, 2, 4), (2, 2, 4), (2, 2, 2), (2, 2, 2), (), (16,),
            (16,), (16,), (16,), (16,), (16,), (16,), (4, 8), (4, 8), (4, 8), (4, 8), (4,), (16, 4),
            (16,), (), (16,), (16,), (16,), (16,)]
    wout, en = pl.pallas_call(
        kernel,
        out_shape=(jax.ShapeDtypeStruct((64, 200), BF16), jax.ShapeDtypeStruct((16,), F32)),
        in_specs=[hbm, hbm, hbm, hbm, vm, vm],
        out_specs=(vm, vm),
        scratch_shapes=[
            pltpu.VMEM((64, 64, 200), BF16),
            pltpu.VMEM((64, 64, 1024), BF16),
            pltpu.VMEM((16, 64, 200), BF16),
            pltpu.VMEM((16, 4096), F32),
            pltpu.VMEM((8, 16, 64, 200), BF16),
            pltpu.VMEM((16, 64, 896), BF16),
            pltpu.VMEM((2, 16, 64, 896), BF16),
            pltpu.VMEM((2, 800, 1024), BF16),
            pltpu.VMEM((16, 16, 128), F32),
            pltpu.VMEM((256, 1024), BF16),
            pltpu.VMEM((4, 2, 8, TILE, 1024), BF16),
            pltpu.VMEM((4, 8, TILE, 1024), BF16),
            pltpu.VMEM((4, 8, TILE, 1024), BF16),
            pltpu.VMEM((4, 8, TILE, 1024), BF16),
            pltpu.VMEM((16, 4, TILE, 1024), BF16),
            pltpu.VMEM((4, TILE, 1024), BF16),
            pltpu.VMEM((16, 64, 200), BF16),
            pltpu.VMEM((2, 1024, 200), BF16),
            pltpu.VMEM((1024, 200), F32),
            pltpu.VMEM((16, 64, 200), BF16),
            pltpu.VMEM((64, 200), BF16),
            pltpu.VMEM((8, 256, 200), BF16),
            pltpu.VMEM((200, 2048), BF16),
            pltpu.VMEM((16, 8, 128), F32),
            pltpu.VMEM((16, 8, 128), F32),
        ] + [dma(s) if s else dma for s in sems],
        compiler_params=pltpu.CompilerParams(
            collective_id=0, has_side_effects=True, vmem_limit_bytes=56 << 20),
        cost_estimate=pl.CostEstimate(flops=14 * 10**9, bytes_accessed=12 * 10**6, transcendentals=0),
    )(
        flip(phi_walkers)[0],
        flip(theta_half),
        chol_vectors,
        flip(chol_rotated),
        flip(hcore_rotated),
        aux_fields,
    )
    return flip(wout)[None], en


def solution(mesh):
    return jax.shard_map(
        body,
        mesh=mesh,
        in_specs=(
            P("chol", None, "orb"),
            P(None, None, "orb"),
            P("chol", "orb", None),
            P("chol", None, "orb"),
            P(None, "orb"),
            P(None, "chol"),
        ),
        out_specs=(P("chol", None, "orb"), P()),
        check_vma=False,
    )
```

```python
import jax
import jax.numpy as jnp
from jax import lax
from jax.experimental import pallas as pl
from jax.experimental.pallas import tpu as pltpu
from jax.sharding import PartitionSpec as P

ORDER = 4
MESH = pl.DeviceIdType.MESH
F32 = jnp.float32
BF16 = jnp.bfloat16
VECTORS = 1024
TILE = 16


def iota(shape, dim):
    return lax.broadcasted_iota(jnp.int32, shape, dim)


def kernel(phi, th, cv, cr, hc, aux, wout, en,
           crv, cvv, thv, zsum, tbuf, pk, abuf, a_t, fbx, smat, opart, osib, osum, opl, obuf, ored,
           pbuf, term, acc, res, land, x_up, x_lo, ebuf, e2buf,
           s_loc, s_cv, s_t1, r_t1, s_tx, r_tx, s_ty, r_ty, s_tf, r_tf, s_phi, r_phi,
           s_a, r_a, s_as, r_as, s_fb, r_fb, s_os, r_os, s_op, r_op, s_od, r_od,
           s_w, r_w, s_e1, r_e1, s_e2, r_e2):
    c = lax.axis_index("chol")
    o = lax.axis_index("orb")
    core = lax.rem(c, 2)
    xl = c // 8
    y = lax.rem(c // 2, 4)
    j = c // 2
    sib = (2 * j + 1 - core, o)
    yp = lax.rem(y + 1, 4)
    ym = lax.rem(y + 3, 4)
    y2 = lax.rem(y + 2, 4)

    def plane(jj):
        return (2 * jj + core, o)

    xpart = plane((1 - xl) * 4 + y)
    dest = core * 8 + lax.rem(2 * y + xl + 4 * core, 8)

    def rcopy(src, dst, ss, rs, dev):
        return pltpu.make_async_remote_copy(
            src_ref=src, dst_ref=dst, send_sem=ss, recv_sem=rs, device_id=dev, device_id_type=MESH)

    def orb_peer(i):
        return lax.rem(o + i, 16)

    def plane_peer(i):
        return lax.rem(j + i, 8)

    cp_cr = pltpu.make_async_copy(cr, crv, s_loc.at[0])
    cp_cr.start()
    cp_th = pltpu.make_async_copy(th, thv, s_loc.at[1])
    cp_th.start()

    def cv_copy(q):
        return pltpu.make_async_copy(cv.at[pl.ds(8 * q, 8)], cvv.at[pl.ds(8 * q, 8)], s_cv.at[q])

    bar = pltpu.get_barrier_semaphore()

    def sig_orb(i, _):
        pl.semaphore_signal(bar, inc=1, device_id=(c, orb_peer(i)), device_id_type=MESH)
        return 0

    def sig_chol(i, _):
        pl.semaphore_signal(bar, inc=1, device_id=(lax.rem(c + i, 16), o), device_id_type=MESH)
        return 0

    lax.fori_loop(1, 16, sig_orb, 0)
    lax.fori_loop(1, 16, sig_chol, 0)
    pl.semaphore_wait(bar, 30)

    cp_own_t = pltpu.make_async_copy(th.at[c], tbuf.at[j, o], s_loc.at[3])
    cp_own_t.start()

    def z_peer(i):
        return (o // 8) * 8 + lax.rem(o + i, 8)

    def t1(i):
        return rcopy(th.at[c], tbuf.at[j, o], s_t1.at[i], r_t1.at[o], (c, z_peer(i)))

    def t1_start(i, _):
        t1(i).start()
        return 0

    lax.fori_loop(1, 8, t1_start, 0)

    cp_phi = rcopy(phi, pbuf.at[o], s_phi, r_phi.at[o], (c, dest))
    cp_phi_own = pltpu.make_async_copy(phi, pbuf.at[o], s_loc.at[4])

    @pl.when(o != dest)
    def _():
        cp_phi.start()

    @pl.when(o == dest)
    def _():
        cp_phi_own.start()

    def a2a(i):
        p = orb_peer(i)
        return rcopy(pk.at[p], abuf.at[core, o], s_a.at[i], r_a.at[o], (c, p))

    def a2a_start(i, _):
        a2a(i).start()
        return 0

    cp_th.wait()
    cp_cr.wait()

    def cv_start(q, _):
        cv_copy(q).start()
        return 0

    lax.fori_loop(0, 8, cv_start, 0)
    def pack(i, _):
        for v in range(4):
            pk[i, :, 200 * v:200 * v + 200] = crv[4 * i + v]
        pk[i, :, 800:] = jnp.zeros((64, 96), BF16)
        return 0

    lax.fori_loop(0, 16, pack, 0)
    cp_own_a = pltpu.make_async_copy(pk.at[o], abuf.at[core, o], s_loc.at[5])
    cp_own_a.start()

    mask = (iota((64, 512), 0) == lax.rem(iota((64, 512), 1), 64)).astype(F32)

    def fb_step(i, _):
        rhs = crv[pl.ds(8 * i, 8)].reshape(512, 200)
        z = lax.dot_general(thv[...].reshape(1024, 200), rhs, (((1,), (1,)), ((), ())),
                            preferred_element_type=F32)
        zsum[:, pl.ds(pl.multiple_of(512 * i, 512), 512)] = jnp.sum(
            z.reshape(16, 64, 512) * mask[None], axis=1)
        return 0

    lax.fori_loop(0, 4, fb_step, 0)
    cp_own_t.wait()

    def t1x(p):
        return rcopy(tbuf.at[j, p], tbuf.at[j, p], s_t1.at[8 + lax.rem(p, 8)], r_t1.at[p], (c, lax.rem(o + 8, 16)))

    t1x(o).start()

    def t1_wait(i, _):
        p = z_peer(i)
        rcopy(th.at[c], tbuf.at[j, p], s_t1.at[i], r_t1.at[p], (c, p)).wait_recv()
        t1x(p).start()
        return 0

    lax.fori_loop(1, 8, t1_wait, 0)

    lax.fori_loop(4, 8, fb_step, 0)
    z1 = lax.dot_general(thv[...].reshape(1024, 200), hc[...], (((1,), (1,)), ((), ())),
                         preferred_element_type=F32)
    z1 = jnp.sum(z1.reshape(16, 64, 64) * mask[None, :, :64], axis=1)
    one_part = jnp.sum(z1, axis=1, keepdims=True)
    zs = zsum[...]
    hi = zs.astype(BF16)
    lo = (zs - hi.astype(F32)).astype(BF16)
    ind = (iota((4096, 128), 1) == iota((4096, 128), 0) // 64).astype(BF16)
    both = jnp.dot(jnp.concatenate([hi, lo], axis=0), ind, preferred_element_type=F32)
    fbx[o] = (both[:16] + both[16:]
              + jnp.where(iota((16, 128), 1) == 64, one_part, 0.0))

    def fb_copy(i):
        return rcopy(fbx.at[o], fbx.at[o], s_fb.at[i], r_fb.at[o], (c, orb_peer(i)))

    def fb_start(i, _):
        fb_copy(i).start()
        return 0

    lax.fori_loop(1, 16, fb_start, 0)
    lax.fori_loop(1, 16, a2a_start, 0)

    def t1x_wait(i, _):
        t1x(lax.rem(z_peer(i) + 8, 16)).wait_recv()
        return 0

    lax.fori_loop(0, 8, t1x_wait, 0)
    jx = (1 - xl) * 4 + y

    def tx(slot, g):
        piece = tbuf.at[slot, pl.ds(4 * g, 4)]
        return rcopy(piece, piece, s_tx.at[g], r_tx.at[g], xpart)


    def ty(slot, which, up, g):
        to = yp if up else ym
        piece = tbuf.at[slot, pl.ds(4 * g, 4)]
        return rcopy(piece, piece, s_ty.at[which, int(up), g], r_ty.at[which, int(up), g],
                     plane(xl * 4 + to))

    def tx_start(g, _):
        tx(j, g).start()
        ty(j, 0, True, g).start()
        ty(j, 0, False, g).start()
        return 0

    lax.fori_loop(0, 4, tx_start, 0)


    def fb_wait(i, _):
        p = orb_peer(i)
        rcopy(fbx.at[p], fbx.at[p], s_fb.at[i], r_fb.at[p], (c, p)).wait_recv()
        return 0

    lax.fori_loop(1, 16, fb_wait, 0)
    fb_all = jnp.sum(fbx[...], axis=0)
    shifted = (aux[...] - fb_all[:, :64]).astype(BF16)

    row = iota((256, 16), 0)
    ew = (iota((256, 16), 1) == 2 * lax.rem(row // TILE, 8) + row // 128).astype(BF16)
    ea = (iota((64, 1024), 0) == iota((64, 1024), 1) // TILE).astype(BF16)
    spread = jnp.dot(jnp.dot(ew, shifted, preferred_element_type=F32).astype(BF16), ea,
                     preferred_element_type=F32)
    diag = lax.rem(iota((256, 1024), 0), TILE) == lax.rem(iota((256, 1024), 1), TILE)
    smat[...] = jnp.where(diag, spread, 0.0).astype(BF16)

    def cv_wait(q, _):
        cv_copy(q).wait()
        return 0

    lax.fori_loop(0, 8, cv_wait, 0)

    def os_copy(t, q):
        return rcopy(opart.at[t, 1 - core, q], osib.at[t, q], s_os.at[t, q], r_os.at[t, q], sib)

    def op_step(t, _):
        def op_half(h, _):
            cols = pl.ds(pl.multiple_of(h * 256, 256), 256)
            rt = cvv[:, pl.ds(pl.multiple_of(TILE * t, TILE), TILE), cols].reshape(1024, 256)
            opart[t, :, :, :, cols] = jnp.dot(
                smat[...], rt, preferred_element_type=F32).astype(BF16).reshape(2, 8, TILE, 256)
            return 0
        lax.fori_loop(0, 4, op_half, 0)

        def os_start(q, _):
            os_copy(t, q).start()
            return 0
        lax.fori_loop(0, 8, os_start, 0)
        return 0

    lax.fori_loop(0, 4, op_step, 0)

    def ty_start(g, _):
        tx(jx, g).wait_recv()
        ty(jx, 1, True, g).start()
        ty(jx, 1, False, g).start()
        return 0

    lax.fori_loop(0, 4, ty_start, 0)

    def op_copy(t, i):
        jj = plane_peer(i)
        return rcopy(osum.at[t, jj], opl.at[t, j], s_op.at[t, i], r_op.at[t, j], plane(jj))

    def sum_step(t, _):
        def os_wait(q, _):
            os_copy(t, q).wait_recv()
            return 0
        lax.fori_loop(0, 8, os_wait, 0)
        osum[t] = (opart[t, core].astype(F32) + osib[t].astype(F32)).astype(BF16)
        opl[t, j] = osum[t, j]

        def go(i, _):
            op_copy(t, i).start()
            return 0
        lax.fori_loop(1, 8, go, 0)
        return 0

    lax.fori_loop(0, 4, sum_step, 0)
    def tf_slot(which, up):
        return (xl if which == 0 else 1 - xl) * 4 + (ym if up else yp)

    def tf(which, up, g):
        piece = tbuf.at[tf_slot(which, up), pl.ds(4 * g + (0 if up else 8), 4)]
        return rcopy(piece, piece, s_tf.at[which, int(up), g], r_tf.at[which, int(up), g],
                     plane(xl * 4 + (yp if up else ym)))

    def tf_step(which):
        def step(g, _):
            for up in (True, False):
                ty(tf_slot(which, up), which, up, g + (0 if up else 2)).wait_recv()
                tf(which, up, g).start()
            return 0
        lax.fori_loop(0, 2, step, 0)

    tf_step(0)

    tf_step(1)

    def as_copy(p):
        return rcopy(abuf.at[core, p], abuf.at[core, p], s_as.at[p], r_as.at[p], sib)

    cp_own_a.wait()
    as_copy(o).start()

    def a_fwd(i, _):
        p = lax.rem(o - i + 16, 16)
        rcopy(pk.at[p], abuf.at[core, p], s_a.at[i], r_a.at[p], (c, p)).wait_recv()
        as_copy(p).start()
        return 0

    lax.fori_loop(1, 16, a_fwd, 0)

    def as_wait(p, _):
        rcopy(abuf.at[1 - core, p], abuf.at[1 - core, p], s_as.at[p], r_as.at[p], sib).wait_recv()
        return 0

    lax.fori_loop(0, 16, as_wait, 0)

    def tr_step(i, _):
        cols = pl.ds(pl.multiple_of(128 * i, 128), 128)
        for k in range(2):
            blk = abuf[k, pl.ds(2 * i, 2)].reshape(128, 896)
            a_t[k, :, cols] = blk.T[:800]
        return 0

    lax.fori_loop(0, 8, tr_step, 0)
    x_lo[...] = jnp.zeros_like(x_lo)
    x_up[...] = jnp.zeros_like(x_up)
    eye = iota((200, 200), 0) == iota((200, 200), 1)

    def w_step(r, tot):
        q = r // 2
        jj = lax.rem(xl + r, 2) * 4 + lax.rem(y + q + (q // 2) * (5 - 2 * q), 4)
        b = tbuf[jj].reshape(1024, 200)

        def half(h, _):
            x = jnp.dot(a_t[h], b,
                        preferred_element_type=F32).astype(BF16).reshape(4, 200, 200)
            for q in range(4):
                x_up[4 * h + q, :200, :] = x[q]
                x_lo[:, pl.ds(pl.multiple_of(1024 * h, 256) + 256 * q, 200)] = x[q]
            return 0
        lax.fori_loop(0, 2, half, 0)
        d = jnp.dot(x_lo[...], x_up[...].reshape(2048, 200), preferred_element_type=F32)
        value = jnp.sum(jnp.where(eye, d, 0.0))
        return tot + jnp.where(iota((8, 128), 1) == 2 * jj + core, value, 0.0)

    pairs = lax.fori_loop(0, 2, w_step, jnp.zeros((8, 128), F32))

    od_copy = lambda t: rcopy(ored.at[t], obuf.at[o, t], s_od.at[t], r_od.at[o, t], (c, dest))

    def red_step(t, _):
        def w(i, _):
            jj = plane_peer(i)
            rcopy(osum.at[t, jj], opl.at[t, jj], s_op.at[t, i], r_op.at[t, jj], plane(jj)).wait_recv()
            return 0
        lax.fori_loop(1, 8, w, 0)
        tot = opl[t, 0].astype(F32)
        for q in range(1, 8):
            tot = tot + opl[t, q].astype(F32)

        @pl.when(o != dest)
        def _():
            ored[t] = tot.astype(BF16)
            od_copy(t).start()

        @pl.when(o == dest)
        def _():
            obuf[o, t] = tot.astype(BF16)
        return 0

    lax.fori_loop(0, 4, red_step, 0)

    def ty_rest(g, _):
        for which in (0, 1):
            for up in (True, False):
                ty(tf_slot(which, up), which, up, g + (2 if up else 0)).wait_recv()
        return 0

    lax.fori_loop(0, 2, ty_rest, 0)

    pairs = lax.fori_loop(2, 6, w_step, pairs)

    @pl.when(o == dest)
    def _():
        cp_phi_own.wait()

        def w(i, _):
            p = orb_peer(i)
            rcopy(phi, pbuf.at[p], s_phi, r_phi.at[p], (c, dest)).wait_recv()

            def wt(t, _):
                rcopy(ored.at[t], obuf.at[p, t], s_od.at[t], r_od.at[p, t], (c, dest)).wait_recv()
                return 0
            lax.fori_loop(0, 4, wt, 0)
            return 0
        lax.fori_loop(1, 16, w, 0)
        term[0] = pbuf[...].reshape(1024, 200)
        acc[...] = pbuf[...].reshape(1024, 200).astype(F32)
        for degree in range(1, ORDER + 1):
            src, dst = (degree - 1) % 2, degree % 2

            def mm(b, _):
                rows = pl.ds(pl.multiple_of(b * 512, 512), 512)
                lhs = obuf[pl.ds(8 * b, 8)].reshape(512, 1024)
                prod = jnp.dot(lhs, term[src], preferred_element_type=F32)
                new = (prod * (1.0 / degree)).astype(BF16)
                term[dst, rows] = new
                acc[rows] = acc[rows] + new.astype(F32)
                return 0
            lax.fori_loop(0, 2, mm, 0)
        res[...] = acc[...].astype(BF16).reshape(16, 64, 200)

        def send(i, _):
            p = orb_peer(i)
            rcopy(res.at[p], land, s_w.at[i], r_w, (c, p)).start()
            return 0
        lax.fori_loop(1, 16, send, 0)


    def tf_wait(g, _):
        for which in (0, 1):
            for up in (True, False):
                slot = (xl if which == 0 else 1 - xl) * 4 + y2
                piece = tbuf.at[slot, pl.ds(4 * g + (0 if up else 8), 4)]
                rcopy(piece, piece, s_tf.at[which, int(up), g], r_tf.at[which, int(up), g], sib).wait_recv()
        return 0

    lax.fori_loop(0, 2, tf_wait, 0)

    pairs = lax.fori_loop(6, 8, w_step, pairs)

    ebuf[o] = pairs

    def e1(i):
        return rcopy(ebuf.at[o], ebuf.at[o], s_e1.at[i], r_e1.at[o], (c, orb_peer(i)))

    def e1_start(i, _):
        e1(i).start()
        return 0

    for i in range(1, 16):
        e1_start(i, 0)

    def e1_wait(i, _):
        p = orb_peer(i)
        rcopy(ebuf.at[p], ebuf.at[p], s_e1.at[i], r_e1.at[p], (c, p)).wait_recv()
        return 0

    @pl.when(o == dest)
    def _():
        wout[...] = res[o]

    @pl.when(o != dest)
    def _():
        rcopy(land, land, s_w.at[0], r_w, (c, dest)).wait_recv()
        wout[...] = land[...]

    for i in range(1, 16):
        e1_wait(i, 0)
    bias = jnp.where(iota((16, 128), 1) < 64, fb_all, 0.0)
    coulomb = jnp.sum(bias * bias, axis=1, keepdims=True)
    wl = iota((16, 128), 0) == iota((16, 128), 1)
    e_row = jnp.sum(jnp.where(wl, coulomb, 0.0), axis=0, keepdims=True)
    one_row = jnp.sum(jnp.where(wl, fb_all[:, 64:65], 0.0), axis=0, keepdims=True)
    e2buf[c] = e_row - jnp.sum(ebuf[...], axis=0)

    def e2(i):
        return rcopy(e2buf.at[c], e2buf.at[c], s_e2.at[i], r_e2.at[c], (lax.rem(c + i, 16), o))

    def e2_start(i, _):
        e2(i).start()
        return 0

    for i in range(1, 16):
        e2_start(i, 0)

    def e2_wait(i, _):
        p = lax.rem(c + i, 16)
        rcopy(e2buf.at[p], e2buf.at[p], s_e2.at[i], r_e2.at[p], (p, o)).wait_recv()
        return 0

    for i in range(1, 16):
        e2_wait(i, 0)
    en[...] = (one_row + 0.5 / VECTORS * jnp.sum(e2buf[...], axis=0))[0, :16]

    def sent(i, _):
        a2a(i).wait_send()
        fb_copy(i).wait_send()
        e1(i).wait_send()
        e2(i).wait_send()
        return 0

    lax.fori_loop(1, 16, sent, 0)

    def sent_t1(i, _):
        t1(i).wait_send()
        return 0

    lax.fori_loop(1, 8, sent_t1, 0)

    def sent_t1x(i, _):
        t1x(z_peer(i)).wait_send()
        return 0

    lax.fori_loop(0, 8, sent_t1x, 0)

    def sent_as(p, _):
        as_copy(p).wait_send()
        return 0

    lax.fori_loop(0, 16, sent_as, 0)
    def sent_th(g, _):
        tx(j, g).wait_send()
        for up in (True, False):
            ty(j, 0, up, g).wait_send()
            ty(jx, 1, up, g).wait_send()
        return 0

    lax.fori_loop(0, 4, sent_th, 0)

    def sent_tf(g, _):
        for which in (0, 1):
            for up in (True, False):
                tf(which, up, g).wait_send()
        return 0

    lax.fori_loop(0, 2, sent_tf, 0)

    def sent_o(t, _):
        def so(q, _):
            os_copy(t, q).wait_send()
            return 0
        lax.fori_loop(0, 8, so, 0)

        def go(i, _):
            op_copy(t, i).wait_send()
            return 0
        lax.fori_loop(1, 8, go, 0)
        return 0

    lax.fori_loop(0, 4, sent_o, 0)

    @pl.when(o != dest)
    def _():
        cp_phi.wait_send()

        def go(t, _):
            od_copy(t).wait_send()
            return 0
        lax.fori_loop(0, 4, go, 0)

    @pl.when(o == dest)
    def _():
        def go(i, _):
            p = orb_peer(i)
            rcopy(res.at[p], land, s_w.at[i], r_w, (c, p)).wait_send()
            return 0
        lax.fori_loop(1, 16, go, 0)


def body(phi_walkers, theta_half, chol_vectors, chol_rotated, hcore_rotated, aux_fields):
    flip = lambda v: jnp.swapaxes(v, -1, -2)
    vm = pl.BlockSpec(memory_space=pltpu.VMEM)
    hbm = pl.BlockSpec(memory_space=pl.ANY)
    dma = pltpu.SemaphoreType.DMA
    sems = [(6,), (8,), (16,), (16,), (4,), (4,), (2, 2, 4), (2, 2, 4), (2, 2, 2), (2, 2, 2), (), (16,),
            (16,), (16,), (16,), (16,), (16,), (16,), (4, 8), (4, 8), (4, 8), (4, 8), (4,), (16, 4),
            (16,), (), (16,), (16,), (16,), (16,)]
    wout, en = pl.pallas_call(
        kernel,
        out_shape=(jax.ShapeDtypeStruct((64, 200), BF16), jax.ShapeDtypeStruct((16,), F32)),
        in_specs=[hbm, hbm, hbm, hbm, vm, vm],
        out_specs=(vm, vm),
        scratch_shapes=[
            pltpu.VMEM((64, 64, 200), BF16),
            pltpu.VMEM((64, 64, 1024), BF16),
            pltpu.VMEM((16, 64, 200), BF16),
            pltpu.VMEM((16, 4096), F32),
            pltpu.VMEM((8, 16, 64, 200), BF16),
            pltpu.VMEM((16, 64, 896), BF16),
            pltpu.VMEM((2, 16, 64, 896), BF16),
            pltpu.VMEM((2, 800, 1024), BF16),
            pltpu.VMEM((16, 16, 128), F32),
            pltpu.VMEM((256, 1024), BF16),
            pltpu.VMEM((4, 2, 8, TILE, 1024), BF16),
            pltpu.VMEM((4, 8, TILE, 1024), BF16),
            pltpu.VMEM((4, 8, TILE, 1024), BF16),
            pltpu.VMEM((4, 8, TILE, 1024), BF16),
            pltpu.VMEM((16, 4, TILE, 1024), BF16),
            pltpu.VMEM((4, TILE, 1024), BF16),
            pltpu.VMEM((16, 64, 200), BF16),
            pltpu.VMEM((2, 1024, 200), BF16),
            pltpu.VMEM((1024, 200), F32),
            pltpu.VMEM((16, 64, 200), BF16),
            pltpu.VMEM((64, 200), BF16),
            pltpu.VMEM((8, 256, 200), BF16),
            pltpu.VMEM((200, 2048), BF16),
            pltpu.VMEM((16, 8, 128), F32),
            pltpu.VMEM((16, 8, 128), F32),
        ] + [dma(s) if s else dma for s in sems],
        compiler_params=pltpu.CompilerParams(
            collective_id=0, has_side_effects=True, vmem_limit_bytes=56 << 20),
        cost_estimate=pl.CostEstimate(flops=14 * 10**9, bytes_accessed=12 * 10**6, transcendentals=0),
    )(
        flip(phi_walkers)[0],
        flip(theta_half),
        chol_vectors,
        flip(chol_rotated),
        flip(hcore_rotated),
        aux_fields,
    )
    return flip(wout)[None], en


def solution(mesh):
    return jax.shard_map(
        body,
        mesh=mesh,
        in_specs=(
            P("chol", None, "orb"),
            P(None, None, "orb"),
            P("chol", "orb", None),
            P("chol", None, "orb"),
            P(None, "orb"),
            P(None, "chol"),
        ),
        out_specs=(P("chol", None, "orb"), P()),
        check_vma=False,
    )
```

```python
import jax
import jax.numpy as jnp
from jax import lax
from jax.experimental import pallas as pl
from jax.experimental.pallas import tpu as pltpu
from jax.sharding import PartitionSpec as P

ORDER = 4
MESH = pl.DeviceIdType.MESH
F32 = jnp.float32
BF16 = jnp.bfloat16
VECTORS = 1024
TILE = 16


def iota(shape, dim):
    return lax.broadcasted_iota(jnp.int32, shape, dim)


def kernel(phi, th, cv, cr, hc, aux, wout, en,
           crv, cvv, thv, zsum, tbuf, pk, abuf, a_t, fbx, smat, opart, osib, osum, opl, obuf, ored,
           pbuf, term, acc, res, land, x_up, x_lo, ebuf, e2buf,
           s_loc, s_cv, s_t1, r_t1, s_tx, r_tx, s_ty, r_ty, s_tf, r_tf, s_phi, r_phi,
           s_a, r_a, s_as, r_as, s_fb, r_fb, s_os, r_os, s_op, r_op, s_od, r_od,
           s_w, r_w, s_e1, r_e1, s_e2, r_e2):
    c = lax.axis_index("chol")
    o = lax.axis_index("orb")
    core = lax.rem(c, 2)
    xl = c // 8
    y = lax.rem(c // 2, 4)
    j = c // 2
    sib = (2 * j + 1 - core, o)
    yp = lax.rem(y + 1, 4)
    ym = lax.rem(y + 3, 4)
    y2 = lax.rem(y + 2, 4)

    def plane(jj):
        return (2 * jj + core, o)

    xpart = plane((1 - xl) * 4 + y)
    dest = core * 8 + lax.rem(2 * y + xl + 4 * core, 8)

    def rcopy(src, dst, ss, rs, dev):
        return pltpu.make_async_remote_copy(
            src_ref=src, dst_ref=dst, send_sem=ss, recv_sem=rs, device_id=dev, device_id_type=MESH)

    def orb_peer(i):
        return lax.rem(o + i, 16)

    def plane_peer(i):
        return lax.rem(j + i, 8)

    cp_cr = pltpu.make_async_copy(cr, crv, s_loc.at[0])
    cp_cr.start()
    cp_th = pltpu.make_async_copy(th, thv, s_loc.at[1])
    cp_th.start()

    def cv_copy(q):
        return pltpu.make_async_copy(cv.at[pl.ds(8 * q, 8)], cvv.at[pl.ds(8 * q, 8)], s_cv.at[q])

    bar = pltpu.get_barrier_semaphore()

    def sig_orb(i, _):
        pl.semaphore_signal(bar, inc=1, device_id=(c, orb_peer(i)), device_id_type=MESH)
        return 0

    def sig_chol(i, _):
        pl.semaphore_signal(bar, inc=1, device_id=(lax.rem(c + i, 16), o), device_id_type=MESH)
        return 0

    lax.fori_loop(1, 16, sig_orb, 0)
    lax.fori_loop(1, 16, sig_chol, 0)
    pl.semaphore_wait(bar, 30)

    cp_own_t = pltpu.make_async_copy(th.at[c], tbuf.at[j, o], s_loc.at[3])
    cp_own_t.start()

    def z_peer(i):
        return (o // 8) * 8 + lax.rem(o + i, 8)

    def t1(i):
        return rcopy(th.at[c], tbuf.at[j, o], s_t1.at[i], r_t1.at[o], (c, z_peer(i)))

    def t1_start(i, _):
        t1(i).start()
        return 0

    lax.fori_loop(1, 8, t1_start, 0)

    cp_phi = rcopy(phi, pbuf.at[o], s_phi, r_phi.at[o], (c, dest))
    cp_phi_own = pltpu.make_async_copy(phi, pbuf.at[o], s_loc.at[4])

    @pl.when(o != dest)
    def _():
        cp_phi.start()

    @pl.when(o == dest)
    def _():
        cp_phi_own.start()

    def a2a(i):
        p = orb_peer(i)
        return rcopy(pk.at[p], abuf.at[core, o], s_a.at[i], r_a.at[o], (c, p))

    def a2a_start(i, _):
        a2a(i).start()
        return 0

    cp_th.wait()
    cp_cr.wait()

    def cv_start(q, _):
        cv_copy(q).start()
        return 0

    lax.fori_loop(0, 8, cv_start, 0)
    def pack(i, _):
        for v in range(4):
            pk[i, :, 200 * v:200 * v + 200] = crv[4 * i + v]
        pk[i, :, 800:] = jnp.zeros((64, 96), BF16)
        return 0

    lax.fori_loop(0, 16, pack, 0)
    cp_own_a = pltpu.make_async_copy(pk.at[o], abuf.at[core, o], s_loc.at[5])
    cp_own_a.start()

    mask = (iota((64, 512), 0) == lax.rem(iota((64, 512), 1), 64)).astype(F32)

    def fb_step(i, _):
        rhs = crv[pl.ds(8 * i, 8)].reshape(512, 200)
        z = lax.dot_general(thv[...].reshape(1024, 200), rhs, (((1,), (1,)), ((), ())),
                            preferred_element_type=F32)
        zsum[:, pl.ds(pl.multiple_of(512 * i, 512), 512)] = jnp.sum(
            z.reshape(16, 64, 512) * mask[None], axis=1)
        return 0

    lax.fori_loop(0, 4, fb_step, 0)
    cp_own_t.wait()

    def t1x(p):
        return rcopy(tbuf.at[j, p], tbuf.at[j, p], s_t1.at[8 + lax.rem(p, 8)], r_t1.at[p], (c, lax.rem(o + 8, 16)))

    t1x(o).start()

    def t1_wait(i, _):
        p = z_peer(i)
        rcopy(th.at[c], tbuf.at[j, p], s_t1.at[i], r_t1.at[p], (c, p)).wait_recv()
        t1x(p).start()
        return 0

    lax.fori_loop(1, 8, t1_wait, 0)

    lax.fori_loop(4, 8, fb_step, 0)
    z1 = lax.dot_general(thv[...].reshape(1024, 200), hc[...], (((1,), (1,)), ((), ())),
                         preferred_element_type=F32)
    z1 = jnp.sum(z1.reshape(16, 64, 64) * mask[None, :, :64], axis=1)
    one_part = jnp.sum(z1, axis=1, keepdims=True)
    zs = zsum[...]
    hi = zs.astype(BF16)
    lo = (zs - hi.astype(F32)).astype(BF16)
    ind = (iota((4096, 128), 1) == iota((4096, 128), 0) // 64).astype(BF16)
    both = jnp.dot(jnp.concatenate([hi, lo], axis=0), ind, preferred_element_type=F32)
    fbx[o] = (both[:16] + both[16:]
              + jnp.where(iota((16, 128), 1) == 64, one_part, 0.0))

    def fb_copy(i):
        return rcopy(fbx.at[o], fbx.at[o], s_fb.at[i], r_fb.at[o], (c, orb_peer(i)))

    def fb_start(i, _):
        fb_copy(i).start()
        return 0

    lax.fori_loop(1, 16, fb_start, 0)
    lax.fori_loop(1, 16, a2a_start, 0)

    def t1x_wait(i, _):
        t1x(lax.rem(z_peer(i) + 8, 16)).wait_recv()
        return 0

    lax.fori_loop(0, 8, t1x_wait, 0)
    jx = (1 - xl) * 4 + y

    def tx(slot, g):
        piece = tbuf.at[slot, pl.ds(4 * g, 4)]
        return rcopy(piece, piece, s_tx.at[g], r_tx.at[g], xpart)


    def ty(slot, which, up, g):
        to = yp if up else ym
        piece = tbuf.at[slot, pl.ds(4 * g, 4)]
        return rcopy(piece, piece, s_ty.at[which, int(up), g], r_ty.at[which, int(up), g],
                     plane(xl * 4 + to))

    def tx_start(g, _):
        tx(j, g).start()
        ty(j, 0, True, g).start()
        ty(j, 0, False, g).start()
        return 0

    lax.fori_loop(0, 4, tx_start, 0)


    def fb_wait(i, _):
        p = orb_peer(i)
        rcopy(fbx.at[p], fbx.at[p], s_fb.at[i], r_fb.at[p], (c, p)).wait_recv()
        return 0

    lax.fori_loop(1, 16, fb_wait, 0)
    fb_all = jnp.sum(fbx[...], axis=0)
    shifted = (aux[...] - fb_all[:, :64]).astype(BF16)

    row = iota((256, 16), 0)
    ew = (iota((256, 16), 1) == 2 * lax.rem(row // TILE, 8) + row // 128).astype(BF16)
    ea = (iota((64, 1024), 0) == iota((64, 1024), 1) // TILE).astype(BF16)
    spread = jnp.dot(jnp.dot(ew, shifted, preferred_element_type=F32).astype(BF16), ea,
                     preferred_element_type=F32)
    diag = lax.rem(iota((256, 1024), 0), TILE) == lax.rem(iota((256, 1024), 1), TILE)
    smat[...] = jnp.where(diag, spread, 0.0).astype(BF16)

    def cv_wait(q, _):
        cv_copy(q).wait()
        return 0

    lax.fori_loop(0, 8, cv_wait, 0)

    def os_copy(t, q):
        return rcopy(opart.at[t, 1 - core, q], osib.at[t, q], s_os.at[t, q], r_os.at[t, q], sib)

    def op_step(t, _):
        def op_half(h, _):
            cols = pl.ds(pl.multiple_of(h * 256, 256), 256)
            rt = cvv[:, pl.ds(pl.multiple_of(TILE * t, TILE), TILE), cols].reshape(1024, 256)
            opart[t, :, :, :, cols] = jnp.dot(
                smat[...], rt, preferred_element_type=F32).astype(BF16).reshape(2, 8, TILE, 256)
            return 0
        lax.fori_loop(0, 4, op_half, 0)

        def os_start(q, _):
            os_copy(t, q).start()
            return 0
        lax.fori_loop(0, 8, os_start, 0)
        return 0

    lax.fori_loop(0, 4, op_step, 0)

    def ty_start(g, _):
        tx(jx, g).wait_recv()
        ty(jx, 1, True, g).start()
        ty(jx, 1, False, g).start()
        return 0

    lax.fori_loop(0, 4, ty_start, 0)

    def op_copy(t, i):
        jj = plane_peer(i)
        return rcopy(osum.at[t, jj], opl.at[t, j], s_op.at[t, i], r_op.at[t, j], plane(jj))

    def sum_step(t, _):
        def os_wait(q, _):
            os_copy(t, q).wait_recv()
            return 0
        lax.fori_loop(0, 8, os_wait, 0)
        osum[t] = (opart[t, core].astype(F32) + osib[t].astype(F32)).astype(BF16)
        opl[t, j] = osum[t, j]

        def go(i, _):
            op_copy(t, i).start()
            return 0
        lax.fori_loop(1, 8, go, 0)
        return 0

    lax.fori_loop(0, 4, sum_step, 0)
    def tf_slot(which, up):
        return (xl if which == 0 else 1 - xl) * 4 + (ym if up else yp)

    def tf(which, up, g):
        piece = tbuf.at[tf_slot(which, up), pl.ds(4 * g + (0 if up else 8), 4)]
        return rcopy(piece, piece, s_tf.at[which, int(up), g], r_tf.at[which, int(up), g],
                     plane(xl * 4 + (yp if up else ym)))

    def tf_step(which):
        def step(g, _):
            for up in (True, False):
                ty(tf_slot(which, up), which, up, g + (0 if up else 2)).wait_recv()
                tf(which, up, g).start()
            return 0
        lax.fori_loop(0, 2, step, 0)

    tf_step(0)

    tf_step(1)

    def as_copy(p):
        return rcopy(abuf.at[core, p], abuf.at[core, p], s_as.at[p], r_as.at[p], sib)

    cp_own_a.wait()
    as_copy(o).start()

    def a_fwd(i, _):
        p = lax.rem(o - i + 16, 16)
        rcopy(pk.at[p], abuf.at[core, p], s_a.at[i], r_a.at[p], (c, p)).wait_recv()
        as_copy(p).start()
        return 0

    lax.fori_loop(1, 16, a_fwd, 0)

    def as_wait(p, _):
        rcopy(abuf.at[1 - core, p], abuf.at[1 - core, p], s_as.at[p], r_as.at[p], sib).wait_recv()
        return 0

    lax.fori_loop(0, 16, as_wait, 0)

    def tr_step(i, _):
        cols = pl.ds(pl.multiple_of(128 * i, 128), 128)
        for k in range(2):
            blk = abuf[k, pl.ds(2 * i, 2)].reshape(128, 896)
            a_t[k, :, cols] = blk.T[:800]
        return 0

    lax.fori_loop(0, 8, tr_step, 0)
    x_lo[...] = jnp.zeros_like(x_lo)
    x_up[...] = jnp.zeros_like(x_up)
    eye = iota((200, 200), 0) == iota((200, 200), 1)

    def w_step(r, tot):
        q = r // 2
        jj = lax.rem(xl + r, 2) * 4 + lax.rem(y + q + (q // 2) * (5 - 2 * q), 4)
        b = tbuf[jj].reshape(1024, 200)

        def half(h, _):
            x = jnp.dot(a_t[h], b,
                        preferred_element_type=F32).astype(BF16).reshape(4, 200, 200)
            for q in range(4):
                x_up[4 * h + q, :200, :] = x[q]
                x_lo[:, pl.ds(pl.multiple_of(1024 * h, 256) + 256 * q, 200)] = x[q]
            return 0
        lax.fori_loop(0, 2, half, 0)
        d = jnp.dot(x_lo[...], x_up[...].reshape(2048, 200), preferred_element_type=F32)
        value = jnp.sum(jnp.where(eye, d, 0.0))
        return tot + jnp.where(iota((8, 128), 1) == 2 * jj + core, value, 0.0)

    pairs = lax.fori_loop(0, 2, w_step, jnp.zeros((8, 128), F32))

    od_copy = lambda t: rcopy(ored.at[t], obuf.at[o, t], s_od.at[t], r_od.at[o, t], (c, dest))

    def red_step(t, _):
        def w(i, _):
            jj = plane_peer(i)
            rcopy(osum.at[t, jj], opl.at[t, jj], s_op.at[t, i], r_op.at[t, jj], plane(jj)).wait_recv()
            return 0
        lax.fori_loop(1, 8, w, 0)
        tot = opl[t, 0].astype(F32)
        for q in range(1, 8):
            tot = tot + opl[t, q].astype(F32)

        @pl.when(o != dest)
        def _():
            ored[t] = tot.astype(BF16)
            od_copy(t).start()

        @pl.when(o == dest)
        def _():
            obuf[o, t] = tot.astype(BF16)
        return 0

    lax.fori_loop(0, 4, red_step, 0)

    def ty_rest(g, _):
        for which in (0, 1):
            for up in (True, False):
                ty(tf_slot(which, up), which, up, g + (2 if up else 0)).wait_recv()
        return 0

    lax.fori_loop(0, 2, ty_rest, 0)

    pairs = lax.fori_loop(2, 6, w_step, pairs)

    def tf_wait(g, _):
        for which in (0, 1):
            for up in (True, False):
                slot = (xl if which == 0 else 1 - xl) * 4 + y2
                piece = tbuf.at[slot, pl.ds(4 * g + (0 if up else 8), 4)]
                rcopy(piece, piece, s_tf.at[which, int(up), g], r_tf.at[which, int(up), g], sib).wait_recv()
        return 0

    lax.fori_loop(0, 2, tf_wait, 0)

    pairs = lax.fori_loop(6, 8, w_step, pairs)

    ebuf[o] = pairs

    def e1(i):
        return rcopy(ebuf.at[o], ebuf.at[o], s_e1.at[i], r_e1.at[o], (c, orb_peer(i)))

    def e1_start(i, _):
        e1(i).start()
        return 0

    for i in range(1, 16):
        e1_start(i, 0)

    @pl.when(o == dest)
    def _():
        cp_phi_own.wait()

        def w(i, _):
            p = orb_peer(i)
            rcopy(phi, pbuf.at[p], s_phi, r_phi.at[p], (c, dest)).wait_recv()

            def wt(t, _):
                rcopy(ored.at[t], obuf.at[p, t], s_od.at[t], r_od.at[p, t], (c, dest)).wait_recv()
                return 0
            lax.fori_loop(0, 4, wt, 0)
            return 0
        lax.fori_loop(1, 16, w, 0)
        term[0] = pbuf[...].reshape(1024, 200)
        acc[...] = pbuf[...].reshape(1024, 200).astype(F32)
        for degree in range(1, ORDER + 1):
            src, dst = (degree - 1) % 2, degree % 2

            def mm(b, _):
                rows = pl.ds(pl.multiple_of(b * 512, 512), 512)
                lhs = obuf[pl.ds(8 * b, 8)].reshape(512, 1024)
                prod = jnp.dot(lhs, term[src], preferred_element_type=F32)
                new = (prod * (1.0 / degree)).astype(BF16)
                term[dst, rows] = new
                acc[rows] = acc[rows] + new.astype(F32)
                return 0
            lax.fori_loop(0, 2, mm, 0)
        res[...] = acc[...].astype(BF16).reshape(16, 64, 200)

        def send(i, _):
            p = orb_peer(i)
            rcopy(res.at[p], land, s_w.at[i], r_w, (c, p)).start()
            return 0
        lax.fori_loop(1, 16, send, 0)


    def e1_wait(i, _):
        p = orb_peer(i)
        rcopy(ebuf.at[p], ebuf.at[p], s_e1.at[i], r_e1.at[p], (c, p)).wait_recv()
        return 0

    for i in range(1, 16):
        e1_wait(i, 0)
    bias = jnp.where(iota((16, 128), 1) < 64, fb_all, 0.0)
    coulomb = jnp.sum(bias * bias, axis=1, keepdims=True)
    wl = iota((16, 128), 0) == iota((16, 128), 1)
    e_row = jnp.sum(jnp.where(wl, coulomb, 0.0), axis=0, keepdims=True)
    one_row = jnp.sum(jnp.where(wl, fb_all[:, 64:65], 0.0), axis=0, keepdims=True)
    e2buf[c] = e_row - jnp.sum(ebuf[...], axis=0)

    def e2(i):
        return rcopy(e2buf.at[c], e2buf.at[c], s_e2.at[i], r_e2.at[c], (lax.rem(c + i, 16), o))

    def e2_start(i, _):
        e2(i).start()
        return 0

    for i in range(1, 16):
        e2_start(i, 0)

    def e2_wait(i, _):
        p = lax.rem(c + i, 16)
        rcopy(e2buf.at[p], e2buf.at[p], s_e2.at[i], r_e2.at[p], (p, o)).wait_recv()
        return 0

    for i in range(1, 16):
        e2_wait(i, 0)
    en[...] = (one_row + 0.5 / VECTORS * jnp.sum(e2buf[...], axis=0))[0, :16]

    @pl.when(o == dest)
    def _():
        wout[...] = res[o]

    @pl.when(o != dest)
    def _():
        rcopy(land, land, s_w.at[0], r_w, (c, dest)).wait_recv()
        wout[...] = land[...]

    def sent(i, _):
        a2a(i).wait_send()
        fb_copy(i).wait_send()
        e1(i).wait_send()
        e2(i).wait_send()
        return 0

    lax.fori_loop(1, 16, sent, 0)

    def sent_t1(i, _):
        t1(i).wait_send()
        return 0

    lax.fori_loop(1, 8, sent_t1, 0)

    def sent_t1x(i, _):
        t1x(z_peer(i)).wait_send()
        return 0

    lax.fori_loop(0, 8, sent_t1x, 0)

    def sent_as(p, _):
        as_copy(p).wait_send()
        return 0

    lax.fori_loop(0, 16, sent_as, 0)
    def sent_th(g, _):
        tx(j, g).wait_send()
        for up in (True, False):
            ty(j, 0, up, g).wait_send()
            ty(jx, 1, up, g).wait_send()
        return 0

    lax.fori_loop(0, 4, sent_th, 0)

    def sent_tf(g, _):
        for which in (0, 1):
            for up in (True, False):
                tf(which, up, g).wait_send()
        return 0

    lax.fori_loop(0, 2, sent_tf, 0)

    def sent_o(t, _):
        def so(q, _):
            os_copy(t, q).wait_send()
            return 0
        lax.fori_loop(0, 8, so, 0)

        def go(i, _):
            op_copy(t, i).wait_send()
            return 0
        lax.fori_loop(1, 8, go, 0)
        return 0

    lax.fori_loop(0, 4, sent_o, 0)

    @pl.when(o != dest)
    def _():
        cp_phi.wait_send()

        def go(t, _):
            od_copy(t).wait_send()
            return 0
        lax.fori_loop(0, 4, go, 0)

    @pl.when(o == dest)
    def _():
        def go(i, _):
            p = orb_peer(i)
            rcopy(res.at[p], land, s_w.at[i], r_w, (c, p)).wait_send()
            return 0
        lax.fori_loop(1, 16, go, 0)


def body(phi_walkers, theta_half, chol_vectors, chol_rotated, hcore_rotated, aux_fields):
    flip = lambda v: jnp.swapaxes(v, -1, -2)
    vm = pl.BlockSpec(memory_space=pltpu.VMEM)
    hbm = pl.BlockSpec(memory_space=pl.ANY)
    dma = pltpu.SemaphoreType.DMA
    sems = [(6,), (8,), (16,), (16,), (4,), (4,), (2, 2, 4), (2, 2, 4), (2, 2, 2), (2, 2, 2), (), (16,),
            (16,), (16,), (16,), (16,), (16,), (16,), (4, 8), (4, 8), (4, 8), (4, 8), (4,), (16, 4),
            (16,), (), (16,), (16,), (16,), (16,)]
    wout, en = pl.pallas_call(
        kernel,
        out_shape=(jax.ShapeDtypeStruct((64, 200), BF16), jax.ShapeDtypeStruct((16,), F32)),
        in_specs=[hbm, hbm, hbm, hbm, vm, vm],
        out_specs=(vm, vm),
        scratch_shapes=[
            pltpu.VMEM((64, 64, 200), BF16),
            pltpu.VMEM((64, 64, 1024), BF16),
            pltpu.VMEM((16, 64, 200), BF16),
            pltpu.VMEM((16, 4096), F32),
            pltpu.VMEM((8, 16, 64, 200), BF16),
            pltpu.VMEM((16, 64, 896), BF16),
            pltpu.VMEM((2, 16, 64, 896), BF16),
            pltpu.VMEM((2, 800, 1024), BF16),
            pltpu.VMEM((16, 16, 128), F32),
            pltpu.VMEM((256, 1024), BF16),
            pltpu.VMEM((4, 2, 8, TILE, 1024), BF16),
            pltpu.VMEM((4, 8, TILE, 1024), BF16),
            pltpu.VMEM((4, 8, TILE, 1024), BF16),
            pltpu.VMEM((4, 8, TILE, 1024), BF16),
            pltpu.VMEM((16, 4, TILE, 1024), BF16),
            pltpu.VMEM((4, TILE, 1024), BF16),
            pltpu.VMEM((16, 64, 200), BF16),
            pltpu.VMEM((2, 1024, 200), BF16),
            pltpu.VMEM((1024, 200), F32),
            pltpu.VMEM((16, 64, 200), BF16),
            pltpu.VMEM((64, 200), BF16),
            pltpu.VMEM((8, 256, 200), BF16),
            pltpu.VMEM((200, 2048), BF16),
            pltpu.VMEM((16, 8, 128), F32),
            pltpu.VMEM((16, 8, 128), F32),
        ] + [dma(s) if s else dma for s in sems],
        compiler_params=pltpu.CompilerParams(
            collective_id=0, has_side_effects=True, vmem_limit_bytes=56 << 20),
        cost_estimate=pl.CostEstimate(flops=14 * 10**9, bytes_accessed=12 * 10**6, transcendentals=0),
    )(
        flip(phi_walkers)[0],
        flip(theta_half),
        chol_vectors,
        flip(chol_rotated),
        flip(hcore_rotated),
        aux_fields,
    )
    return flip(wout)[None], en


def solution(mesh):
    return jax.shard_map(
        body,
        mesh=mesh,
        in_specs=(
            P("chol", None, "orb"),
            P(None, None, "orb"),
            P("chol", "orb", None),
            P("chol", None, "orb"),
            P(None, "orb"),
            P(None, "chol"),
        ),
        out_specs=(P("chol", None, "orb"), P()),
        check_vma=False,
    )
```
